32 devices in a mesh: rows: 16 (over z, y, x), rhs: 2 (over core).
Axes of the slice: x: 2, y: 2, z: 4, core: 2. Of those that a mesh axis runs over, the one named last changes fastest.
Arguments:
- right_side: float32 [64, 8192], P('rhs', 'rows'), may hold values from -6 to 6
- tiles: float32 [128, 7, 64, 64], P('rows'), may hold values from -2 to 5.5, as said below
- pivots: float32 [128, 64, 64], P('rows'), may hold values from -0.05 to 0.8, as said below
- columns: int32 [128, 7], P('rows'), may hold values from 0 to 127, as said below
Outputs:
- solution: float32 [64, 8192], P('rhs', 'rows')
- residual: float32 [64, 8192], P('rhs', 'rows')
The draws below stay inside these ranges and needn't reach their ends.
Inputs may be any that keep to these rules, and one draw needn't show every extreme that they name: columns[i, 0] = i. The other six columns of block row i are i - o and i + o for three offsets o shared by all block rows, the largest of them exactly 8, in an order of the slots drawn for each block row; a column that would fall outside 0 to 127 is i itself. tiles[i, 0] is the diagonal tile of block row i; A is symmetric positive definite: the tile of block row i in a slot whose column j differs from i is the transpose of the tile of block row j in its slot whose column is i. Every pivots[i] is symmetric positive definite.
All inputs are finite; a program needn't handle non-finite values.
Results may differ from the reference program's by a relative error of at most 0.0003.
Values sent between devices are 32-bit elements; how exact they have to be, the bound alone decides.
No kernel may reach another device: no remote copies, remote signals or barrier semaphores. Data moves between devices by JAX's collectives and lax.ppermute only.
A program may use at most 64 MiB of HBM per device.

```python
import math
import jax
import jax.numpy as jnp
from jax import lax

BS = 64
RHS = 64
TILES = 7
BR_DEV = 8
SPAN = 8
ITERS = 2
NBR = 128


def pattern(key):
    first = jax.random.randint(jax.random.fold_in(key, 11), (), 1, BR_DEV // 2 + 1)
    second = jax.random.randint(jax.random.fold_in(key, 12), (), BR_DEV // 2 + 1, BR_DEV)
    offsets = jnp.stack([first, second, jnp.asarray(BR_DEV, jnp.int32)]).astype(jnp.int32)
    scores = jax.random.randint(jax.random.fold_in(key, 13), (NBR, 6), 0, 1 << 20) * 8
    scores = scores + jnp.arange(6, dtype=jnp.int32)[None]
    kinds = jnp.argsort(scores, axis=1).astype(jnp.int32)
    kind_type = kinds // 2
    upward = kinds % 2 == 0
    reach = offsets[kind_type]
    rows = jnp.arange(NBR, dtype=jnp.int32)[:, None]
    neighbour = jnp.where(upward, rows + reach, rows - reach)
    inside = (neighbour >= 0) & (neighbour < NBR)
    columns = jnp.concatenate([rows, jnp.where(inside, neighbour, rows)], axis=1).astype(jnp.int32)
    edge_row = jnp.where(upward, rows, rows - reach) % NBR
    return (offsets, kind_type, inside, columns, edge_row)


def couplings(key):
    strong = jnp.exp(jax.random.uniform(jax.random.fold_in(key, 21), (NBR, 1), jnp.float32, 0.0, math.log(2.0)))
    weak = 0.15 * jnp.exp(jax.random.uniform(jax.random.fold_in(key, 22), (NBR, 2), jnp.float32, 0.0, math.log(2.0)))
    mass = 0.05 * jnp.exp(jax.random.uniform(jax.random.fold_in(key, 23), (NBR,), jnp.float32, 0.0, math.log(4.0)))
    return (jnp.concatenate([weak, strong], axis=1), mass)


def symmetric_noise(key, lead):
    bound = 0.9 / (BS - 1)
    shape = lead + (BS, BS)
    raw = bound / 2.0 * jax.random.truncated_normal(key, -2.0, 2.0, shape, jnp.float32)
    sym = 0.5 * (raw + jnp.swapaxes(raw, -1, -2))
    return sym * (1.0 - jnp.eye(BS, dtype=jnp.float32))


def draw_columns(key, part):
    offsets, kind_type, inside, columns, edge_row = pattern(key)
    return columns


def draw_tiles(key, part):
    offsets, kind_type, inside, columns, edge_row = pattern(key)
    strength, mass = couplings(key)
    eye = jnp.eye(BS, dtype=jnp.float32)
    edges = strength[:, :, None, None] * (eye[None, None] + symmetric_noise(jax.random.fold_in(key, 31), (NBR, 3)))
    flat = edges.reshape(NBR * 3, BS, BS)
    index = (edge_row * 3 + kind_type).reshape(-1)
    picked = jnp.take(flat, index, axis=0).reshape(NBR, 6, BS, BS)
    inside_f = inside.astype(jnp.float32)[:, :, None, None]
    outer = picked * (1.0 - 2.0 * inside_f)
    extra = symmetric_noise(jax.random.fold_in(key, 32), (NBR,))
    diagonal = jnp.sum(picked * inside_f, axis=1) + mass[:, None, None] * (eye[None] + extra)
    return jnp.concatenate([diagonal[:, None], outer], axis=1)


def draw_pivots(key, part):
    offsets, kind_type, inside, columns, edge_row = pattern(key)
    strength, mass = couplings(key)
    picked = jnp.take(strength.reshape(-1), edge_row * 3 + kind_type)
    total = jnp.sum(picked, axis=1) + mass
    block_rows = SPAN * BR_DEV
    count_blocks = NBR // block_rows
    total_b = total.reshape(count_blocks, block_rows)
    strength_b = strength.reshape(count_blocks, block_rows, 3)

    def step(place, pivot):
        value = lax.dynamic_index_in_dim(total_b, place, 1, False)
        for kind in range(3):
            earlier = jnp.maximum(place - offsets[kind], 0)
            coupling = lax.dynamic_index_in_dim(strength_b[:, :, kind], earlier, 1, False)
            before = lax.dynamic_index_in_dim(pivot, earlier, 1, False)
            value = value - jnp.where(place >= offsets[kind], coupling * coupling / before, 0.0)
        return lax.dynamic_update_index_in_dim(pivot, value, place, 1)
    pivot = lax.fori_loop(0, block_rows, step, jnp.ones_like(total_b))
    scale = 1.0 / pivot.reshape(NBR)
    eye = jnp.eye(BS, dtype=jnp.float32)
    noise = symmetric_noise(jax.random.fold_in(key, 33), (NBR,))
    return scale[:, None, None] * (eye[None] + noise)


def draw_right_side(key, part):
    shape = (RHS, NBR * BS)
    return jax.random.truncated_normal(jax.random.fold_in(key, 41), -6.0, 6.0, shape, jnp.float32)


def setup_inputs(seed: int = 0) -> dict:
    key_of = jax.random.split(jax.random.key(seed), 5)
    return {
        "right_side": draw_right_side(jax.random.fold_in(key_of[4], 71), 0),
        "tiles": draw_tiles(jax.random.fold_in(key_of[4], 71), 0),
        "pivots": draw_pivots(jax.random.fold_in(key_of[4], 71), 0),
        "columns": draw_columns(jax.random.fold_in(key_of[4], 71), 0),
    }


def inner(left, right):
    return jnp.dot(left, right.T, precision=lax.Precision.HIGHEST)

def chol_solve(factor, values):
    middle = lax.linalg.triangular_solve(factor, values, left_side=True, lower=True)
    return lax.linalg.triangular_solve(factor, middle, left_side=True, lower=True, transpose_a=True)

def reference(right_side, tiles, pivots, columns):
    groups = NBR // BR_DEV

    def product(vector):
        blocks = vector.reshape(RHS, NBR, BS)
        tile_groups = tiles.reshape(groups, BR_DEV, TILES, BS, BS)
        col_groups = columns.reshape(groups, BR_DEV, TILES)

        def one_group(pair):
            group_tiles, group_cols = pair
            picked = jnp.take(blocks, group_cols, axis=1)
            return jnp.einsum('ikab,cikb->cia', group_tiles, picked, precision=lax.Precision.HIGHEST)
        result = lax.map(one_group, (tile_groups, col_groups))
        return jnp.transpose(result, (1, 0, 2, 3)).reshape(RHS, NBR * BS)
    block_rows = SPAN * BR_DEV
    count_blocks = NBR // block_rows
    starts = jnp.arange(count_blocks, dtype=jnp.int32) * block_rows

    def precondition(vector):
        source = vector.reshape(RHS, NBR, BS)

        def forward(turn, lowered):
            rows_now = starts + turn
            cols_now = columns[rows_now]
            keep = (cols_now < rows_now[:, None]) & (cols_now >= starts[:, None])
            masked = tiles[rows_now] * keep[:, :, None, None].astype(tiles.dtype)
            picked = jnp.take(lowered, cols_now, axis=1)
            summed = jnp.einsum('jkab,cjkb->cja', masked, picked, precision=lax.Precision.HIGHEST)
            remain = source[:, rows_now] - summed
            value = jnp.einsum('jab,cjb->cja', pivots[rows_now], remain, precision=lax.Precision.HIGHEST)
            return lowered.at[:, rows_now].set(value)
        lowered = lax.fori_loop(0, block_rows, forward, jnp.zeros_like(source))

        def backward(turn, result):
            rows_now = starts + (block_rows - 1) - turn
            cols_now = columns[rows_now]
            keep = (cols_now > rows_now[:, None]) & (cols_now < (starts + block_rows)[:, None])
            masked = tiles[rows_now] * keep[:, :, None, None].astype(tiles.dtype)
            picked = jnp.take(result, cols_now, axis=1)
            summed = jnp.einsum('jkab,cjkb->cja', masked, picked, precision=lax.Precision.HIGHEST)
            value = lowered[:, rows_now] - jnp.einsum('jab,cjb->cja', pivots[rows_now], summed, precision=lax.Precision.HIGHEST)
            return result.at[:, rows_now].set(value)
        result = lax.fori_loop(0, block_rows, backward, lowered)
        return result.reshape(RHS, NBR * BS)
    solution = jnp.zeros_like(right_side)
    residual = right_side
    direction = precondition(residual)
    for turn in range(ITERS):
        image = product(direction)
        gram = inner(direction, image)
        factor = jnp.linalg.cholesky(0.5 * (gram + gram.T))
        alpha = chol_solve(factor, inner(direction, residual))
        solution = solution + jnp.dot(alpha.T, direction, precision=lax.Precision.HIGHEST)
        residual = residual - jnp.dot(alpha.T, image, precision=lax.Precision.HIGHEST)
        if turn + 1 < ITERS:
            preconditioned = precondition(residual)
            beta = -chol_solve(factor, inner(image, preconditioned))
            direction = preconditioned + jnp.dot(beta.T, direction, precision=lax.Precision.HIGHEST)
    return (solution, residual)
```

```python
import functools
import jax
import jax.numpy as jnp
from jax import lax
from jax.experimental import pallas as pl
from jax.experimental.pallas import tpu as pltpu
from jax.sharding import Mesh, PartitionSpec as P

SPAN = 8
F32 = jnp.float32
BF16 = jnp.bfloat16
HIGHEST = lax.Precision.HIGHEST
NN = (((1,), (0,)), ((), ()))
NT = (((1,), (1,)), ((), ()))
VMEM = pl.BlockSpec(memory_space=pltpu.VMEM)
SMEM = pl.BlockSpec(memory_space=pltpu.SMEM)


def call(kernel, name, out_shape, in_specs, out_specs=VMEM, scratch=(), limit=16):
    return pl.pallas_call(
        kernel,
        out_shape=out_shape,
        in_specs=in_specs,
        out_specs=out_specs,
        scratch_shapes=list(scratch),
        compiler_params=pltpu.CompilerParams(vmem_limit_bytes=limit * 2**20),
        name=name,
    )


def two_parts(x):
    high = x.astype(BF16).astype(F32)
    return jnp.concatenate([high, x - high], axis=0).astype(BF16)


def halves(x):
    high = x.astype(BF16)
    return high, (x - high.astype(F32)).astype(BF16)


def product(x, high, low, dims):
    parts = two_parts(x)
    both = lax.dot_general(parts, high, dims, preferred_element_type=F32)
    both = both + lax.dot_general(parts, low, dims, preferred_element_type=F32)
    rows = x.shape[0]
    return both[:rows] + both[rows:]


def offsets_of(columns, start):
    found = []
    for offset in range(1, 8):
        hit = jnp.int32(0)
        for slot in range(7):
            away = columns[0, slot] - start
            hit = hit | jnp.where((away == offset) | (away == -offset), 1, 0)
        found.append(hit * 16 + offset)
    first = functools.reduce(jnp.maximum, found)
    second = functools.reduce(jnp.maximum, [jnp.where(f == first, 0, f) for f in found])
    first, second = (first & 15, second & 15)
    return (jnp.minimum(first, second), jnp.maximum(first, second), jnp.int32(8))


def pack_kernel(rows_part, columns, tiles, pivots, packed, diagonal, offsets):
    shard_rows = tiles.shape[0]
    start = (lax.axis_index("blk") * SPAN + lax.axis_index("pos")) * shard_rows
    base = lax.axis_index("rhs") * rows_part
    offs = offsets_of(columns, start)
    for k in range(3):
        offsets[0, k] = offs[k]
    for r in range(rows_part):
        row = base + r
        here = start + row
        sums = [jnp.zeros(tiles.shape[2:], F32) for _ in range(4)]
        for slot in range(7):
            away = columns[row, slot] - here
            tile = tiles[row, slot]
            for k, want in enumerate((*offs, 0)):
                sums[k] = sums[k] + tile * jnp.where(away == want, 1.0, 0.0)
        packed[r, 0] = jnp.concatenate([sums[0], sums[1]], axis=1)
        packed[r, 1] = jnp.concatenate([sums[2], pivots[row]], axis=1)
        half = sums[3].shape[0] // 2
        diagonal[r] = jnp.concatenate([sums[3][:half], sums[3][half:]], axis=1)


def band_kernel(columns, tiles, band_high, band_low, band):
    shard_rows, slots, order, _ = tiles.shape
    start = (lax.axis_index("blk") * SPAN + lax.axis_index("pos")) * shard_rows
    band[...] = jnp.zeros_like(band)
    for row in range(shard_rows):
        for slot in range(slots):
            away = columns[row, slot] - start + shard_rows
            where = pl.ds(pl.multiple_of(away * order, order), order)
            lanes = pl.ds(row * order, order)
            band[where, lanes] = band[where, lanes] + tiles[row, slot].T
    high, low = halves(band[...])
    band_high[...] = high
    band_low[...] = low


def factor_kernel(offsets, packed, m_high, m_low, w_high, w_low):
    order = 64
    cells = 8 * order
    o = [offsets[0, k] for k in range(3)]
    m_high[...] = jnp.zeros_like(m_high)
    m_low[...] = jnp.zeros_like(m_low)

    def fill(s, carry):
        for i in range(8):
            for k in range(3):
                from_row = (i - o[k]) & 7
                kind = jnp.where(o[k] > i, 0, 1)
                tile = packed[8 * s + from_row, k // 2, :, (k % 2) * order : (k % 2 + 1) * order]
                high, low = halves(tile)
                where = pl.ds(pl.multiple_of(from_row * order, order), order)
                lanes = pl.ds(i * order, order)
                m_high[s, kind, where, lanes] = high
                m_low[s, kind, where, lanes] = low
        return carry

    lax.fori_loop(0, 8, fill, 0)

    lane = lax.broadcasted_iota(jnp.int32, (order, 2 * order), 1)
    for j in range(7, -1, -1):
        for s in range(8):
            pivot = packed[8 * s + j, 1, :, order:]
            row = jnp.pad(pivot, ((0, 0), (j * order, cells - (j + 1) * order)))
            if j < 7:
                inside = [jnp.where(o[k] + j <= 7, 1.0, 0.0) for k in range(2)]
                pair = packed[8 * s + j, 0] * jnp.where(lane < order, inside[0], inside[1])
                scaled = product(pivot, *halves(pair), NN)
                left = two_parts(scaled)
                left = jnp.concatenate([left, left], axis=1)
                where = [
                    pl.ds(pl.multiple_of(jnp.minimum(o[k] + j, 7) * order, order), order)
                    for k in range(2)
                ]
                first = (j + 1) // 4 * 256
                right = jnp.concatenate(
                    [w[s, where[k], first:] for w in (w_high, w_low) for k in range(2)], axis=0
                )
                both = lax.dot_general(left, right, NN, preferred_element_type=F32)
                away = both[:order] + both[order:]
                if first:
                    away = jnp.pad(away, ((0, 0), (first, 0)))
                row = row - away
            high, low = halves(row)
            w_high[s, j * order : (j + 1) * order] = high
            w_low[s, j * order : (j + 1) * order] = low


def upper(x, high, low):
    half = high.shape[0] // 2
    return jnp.concatenate(
        [
            product(x[:, :half], high[:half, :half], low[:half, :half], NN),
            product(x, high[:, half:], low[:, half:], NN),
        ],
        axis=1,
    )


def upper_t(x, high, low):
    half = high.shape[0] // 2
    return jnp.concatenate(
        [
            product(x, high[:half], low[:half], NT),
            product(x[:, half:], high[half:, half:], low[half:, half:], NT),
        ],
        axis=1,
    )


def lower(x, high, low):
    half = high.shape[0] // 2
    return jnp.concatenate(
        [
            product(x, high[:, :half], low[:, :half], NN),
            product(x[:, half:], high[half:, half:], low[half:, half:], NN),
        ],
        axis=1,
    )


def lower_t(x, high, low):
    half = high.shape[0] // 2
    return jnp.concatenate(
        [
            product(x[:, :half], high[:half, :half], low[:half, :half], NT),
            product(x, high[half:], low[half:], NT),
        ],
        axis=1,
    )


def forward_step(s, source, before, m, w):
    if before is not None:
        source = source - lower(before, m[0].at[s - 1, 0], m[1].at[s - 1, 0])
    value = upper(source, w[0].at[s], w[1].at[s])
    return value, source - upper(value, m[0].at[s, 1], m[1].at[s, 1])


def first_kernel(r, m_high, m_low, w_high, w_low, t, last, coupled):
    m, w = (m_high, m_low), (w_high, w_low)
    value = None
    for s in range(8):
        value, t[s] = forward_step(s, r[s], value, m, w)
    z = upper_t(t[7], w_high.at[7], w_low.at[7])
    last[...] = z
    coupled[...] = lower(z, m_high.at[7, 0], m_low.at[7, 0])


def second_kernel(t, last, m_high, m_low, w_high, w_low, z, above):
    value = last[...]
    z[7] = value
    for s in range(6, -1, -1):
        above[s] = lower_t(value, m_high.at[s, 0], m_low.at[s, 0])
        value = upper_t(t[s] - above[s], w_high.at[s], w_low.at[s])
        z[s] = value


def third_kernel(r, z, above, arrived, diagonal, m_high, m_low, w_high, w_low, image, t, value):
    m, w = (m_high, m_low), (w_high, w_low)
    order = 64
    before = None
    for s in range(8):
        x = z[s]
        total = upper(x, m_high.at[s, 1], m_low.at[s, 1]) + upper_t(x, m_high.at[s, 1], m_low.at[s, 1])
        own = []
        for i in range(8):
            pair = diagonal[8 * s + i]
            tile = jnp.concatenate([pair[:, :order], pair[:, order:]], axis=0)
            own.append(product(x[:, i * order : (i + 1) * order], *halves(tile), NN))
        total = total + jnp.concatenate(own, axis=1)
        if s:
            total = total + lower(z[s - 1], m_high.at[s - 1, 0], m_low.at[s - 1, 0])
        else:
            total = total + arrived[...]
        if s < 7:
            total = total + above[s]
        image[s] = total
        if s < 7:
            before, t[s] = forward_step(s, total - r[s], before, m, w)
    value[...] = before


def fourth_kernel(r, partial, arrived, t, value, m_high, m_low, w_high, w_low, image, out, extra):
    m, w = (m_high, m_low), (w_high, w_low)
    blocks = out.shape[0]
    block = lax.axis_index("blk")
    total = partial[...] + lower_t(arrived[...], m_high.at[7, 0], m_low.at[7, 0])
    image[...] = total
    _, final = forward_step(7, total - r[7], value[...], m, w)
    out[...] = jnp.zeros_like(out)
    y = upper_t(final, w_high.at[7], w_low.at[7])
    extra[7] = y
    for s in range(6, -1, -1):
        y = upper_t(t[s] - lower_t(y, m_high.at[s, 0], m_low.at[s, 0]), w_high.at[s], w_low.at[s])
        extra[s] = y
    for s in range(8):
        for side in range(3):
            group = s + side - 1
            if 0 <= group < 8:
                out[block, s, side] = extra[group]

    @pl.when(block + 1 < blocks)
    def _():
        out[block + 1, 0, 0] = extra[7]

    @pl.when(block > 0)
    def _():
        out[block - 1, 7, 2] = extra[0]


def place_rows(place, t, rhs, rows, lanes=slice(None)):
    count = rows.shape[0]
    place[pl.ds(pl.multiple_of((rhs ^ t) * count, count), count), lanes] = rows


def early_kernel(n, *refs):
    r_pieces, dq_pieces = refs[:n], refs[n : 2 * n]
    r, d, q, sums = refs[2 * n :]
    rhs = lax.axis_index("rhs")
    for t in range(n):
        place_rows(r, t, rhs, r_pieces[t][...])
        for kind, place in enumerate((d, q)):
            rows = jnp.concatenate([dq_pieces[t][j, kind] for j in range(SPAN)], axis=0)
            place_rows(place, t, rhs, rows)
    for k, other in enumerate((r, q)):
        sums[k] = lax.dot_general(
            d[...], other[...], NT, precision=HIGHEST, preferred_element_type=F32
        )


def late_kernel(n, *refs):
    pieces = refs[:n]
    q, band_high, band_low, e, w, sums, wide = refs[n:]
    rhs = lax.axis_index("rhs")
    blocks, _, _, _, cells = pieces[0].shape
    for side in range(3):
        lanes = slice(side * cells, (side + 1) * cells)
        for t, piece in enumerate(pieces):
            rows = [
                sum(piece[block, j, side] for block in range(blocks)) for j in range(SPAN)
            ]
            place_rows(wide, t, rhs, jnp.concatenate(rows, axis=0), lanes)
    e[...] = wide[:, cells : 2 * cells]
    w[...] = product(wide[...], band_high[...], band_low[...], NN)
    for k, other in enumerate((q, w)):
        sums[k] = lax.dot_general(
            e[...], other[...], NT, precision=HIGHEST, preferred_element_type=F32
        )


def small(a, b):
    return lax.dot_general(a, b, NN, precision=HIGHEST, preferred_element_type=F32)


def inverse(a):
    size = a.shape[0]
    row_at = lax.broadcasted_iota(jnp.int32, a.shape, 0)
    col_at = lax.broadcasted_iota(jnp.int32, a.shape, 1)
    for k in range(size):
        scale = 1.0 / a[k : k + 1, k : k + 1]
        row = jnp.where(col_at[:1] == k, 1.0, a[k : k + 1, :]) * scale
        column = a[:, k : k + 1]
        rest = jnp.where(col_at == k, 0.0, a)
        a = jnp.where(row_at == k, row, rest - column * row)
    return a


def symmetric(a):
    return 0.5 * (a + a.T)


def invert_kernel(sums, inverted):
    inverted[...] = inverse(symmetric(sums[1]))


def last_kernel(early, late, inverted, r, d, q, e, w, solution, residual):
    count = solution.shape[0]
    rhs = lax.axis_index("rhs")
    s1, s2 = symmetric(early[0]), symmetric(early[1])
    s3, s4 = symmetric(late[0]), symmetric(late[1])
    inv = inverted[...]
    c = small(inv, s3)
    schur = symmetric(s4 - small(s3, c))
    h = small(s2 - s1 - small(s1, c), inverse(schur))
    f = small(s1 - small(h, s3), inv)
    pick = lax.broadcasted_iota(jnp.int32, (count, s1.shape[0]), 0) + rhs * count
    pick = jnp.where(pick == lax.broadcasted_iota(jnp.int32, pick.shape, 1), 1.0, 0.0)
    f, h = small(pick, f), small(pick, h)
    solution[...] = small(f, d[...]) + small(h, e[...])
    own = r[pl.ds(pl.multiple_of(rhs * count, count), count), :]
    residual[...] = own - small(f, q[...]) - small(h, w[...])


def swapped(value, axis, bit):
    return lax.ppermute(value, axis, [(i, i ^ bit) for i in range(lax.axis_size(axis))])


def summed(value):
    for axis in ("pos", "blk"):
        bit = 1
        while bit < lax.axis_size(axis):
            value = value + swapped(value, axis, bit)
            bit *= 2
    return value


def shards(right_side, tiles, pivots, columns):
    count, cells = right_side.shape
    shard_rows, slots, order, _ = tiles.shape
    parts = lax.axis_size("rhs")
    blocks = lax.axis_size("blk")
    rows_part = shard_rows // parts
    each = count // SPAN
    total = count * parts
    S = jax.ShapeDtypeStruct
    up = [(i, i + 1) for i in range(blocks - 1)]
    down = [(i + 1, i) for i in range(blocks - 1)]

    packed, diagonal, offsets = call(
        functools.partial(pack_kernel, rows_part),
        "pack_tiles",
        [
            S((rows_part, 2, order, 2 * order), F32),
            S((rows_part, order // 2, 2 * order), F32),
            S((1, 3), jnp.int32),
        ],
        [SMEM, VMEM, VMEM],
        [VMEM, VMEM, SMEM],
    )(columns, tiles, pivots)
    packed = lax.all_gather(packed, ("pos", "rhs"), axis=0, tiled=True)
    diagonal = lax.all_gather(diagonal, ("pos", "rhs"), axis=0, tiled=True)
    r = lax.all_to_all(right_side.reshape(SPAN, each, cells), "pos", 0, 0, tiled=True)
    r_pieces = [right_side] + [swapped(right_side, "rhs", t) for t in range(1, parts)]
    band_high, band_low = call(
        band_kernel,
        "row_band",
        [S((3 * cells, cells), BF16)] * 2,
        [SMEM, VMEM],
        [VMEM] * 2,
        [pltpu.VMEM((3 * cells, cells), F32)],
    )(columns, tiles)

    square = pltpu.VMEM((SPAN, 2, cells, cells), BF16)
    single = pltpu.VMEM((SPAN, cells, cells), BF16)
    mats = call(
        factor_kernel,
        "block_factors",
        [square, square, single, single],
        [SMEM, VMEM],
        [VMEM] * 4,
    )(offsets, packed)
    vectors, vector = S((SPAN, each, cells), F32), S((each, cells), F32)
    t, last, coupled = call(
        first_kernel, "forward_r", [vectors, vector, vector], [VMEM] * 5, [VMEM] * 3
    )(r, *mats)
    from_below = lax.ppermute(coupled, "blk", up)
    z, above = call(second_kernel, "backward_r", [vectors] * 2, [VMEM] * 6, [VMEM] * 2)(t, last, *mats)
    from_above = lax.ppermute(z[0], "blk", down)
    image, t, value = call(
        third_kernel, "image_and_forward", [vectors, vectors, vector], [VMEM] * 9, [VMEM] * 3
    )(r, z, above, from_below, diagonal, *mats)
    image_last, y = call(
        fourth_kernel,
        "backward_image",
        [vector, S((blocks, SPAN, 3, each, cells), F32)],
        [VMEM] * 9,
        [VMEM] * 2,
        [pltpu.VMEM((SPAN, each, cells), F32)],
    )(r, image[7], from_above, t, value, *mats)
    image = jnp.concatenate([image[:7], image_last[None]], axis=0)

    dq = lax.all_to_all(jnp.stack([z, image], axis=1), "pos", 0, 0, tiled=True)
    dq_pieces = [dq] + [swapped(dq, "rhs", t) for t in range(1, parts)]
    full, two = S((total, cells), F32), S((2, total, total), F32)
    r_full, d_full, q_full, early = call(
        functools.partial(early_kernel, parts),
        "products_d",
        [full, full, full, two],
        [VMEM] * (2 * parts),
        [VMEM] * 4,
    )(*r_pieces, *dq_pieces)
    early = summed(early)
    inverted = call(invert_kernel, "invert", S((total, total), F32), [VMEM])(early)

    y = lax.all_to_all(
        y.reshape(blocks * SPAN, 3, each, cells), ("blk", "pos"), 0, 0, tiled=True
    ).reshape(blocks, SPAN, 3, each, cells)
    y_pieces = [y] + [swapped(y, "rhs", t) for t in range(1, parts)]
    e_full, w_full, late = call(
        functools.partial(late_kernel, parts),
        "products_e",
        [full, full, two],
        [VMEM] * (parts + 3),
        [VMEM] * 3,
        [pltpu.VMEM((total, 3 * cells), F32)],
    )(*y_pieces, q_full, band_high, band_low)
    late = summed(late)
    return call(
        last_kernel, "update", [S((count, cells), F32)] * 2, [VMEM] * 8, [VMEM] * 2
    )(early, late, inverted, r_full, d_full, q_full, e_full, w_full)


def solution(mesh):
    devices = mesh.devices
    split = Mesh(
        devices.reshape(devices.shape[0] // SPAN, SPAN, devices.shape[1]), ("blk", "pos", "rhs")
    )
    rows = ("blk", "pos")
    return jax.shard_map(
        shards,
        mesh=split,
        in_specs=(
            P("rhs", rows),
            P(rows, None, None, None),
            P(rows, None, None),
            P(rows, None),
        ),
        out_specs=(P("rhs", rows), P("rhs", rows)),
        check_vma=False,
    )
```

```python
import functools
import jax
import jax.numpy as jnp
from jax import lax
from jax.experimental import pallas as pl
from jax.experimental.pallas import tpu as pltpu
from jax.sharding import Mesh, PartitionSpec as P

SPAN = 8
F32 = jnp.float32
BF16 = jnp.bfloat16
HIGHEST = lax.Precision.HIGHEST
NN = (((1,), (0,)), ((), ()))
NT = (((1,), (1,)), ((), ()))
VMEM = pl.BlockSpec(memory_space=pltpu.VMEM)
SMEM = pl.BlockSpec(memory_space=pltpu.SMEM)


def call(kernel, name, out_shape, in_specs, out_specs=VMEM, scratch=(), aliases=None, cost=1):
    return pl.pallas_call(
        kernel,
        out_shape=out_shape,
        in_specs=in_specs,
        out_specs=out_specs,
        scratch_shapes=list(scratch),
        input_output_aliases=aliases or {},
        cost_estimate=pl.CostEstimate(flops=int(cost * 1e9), bytes_accessed=0, transcendentals=0),
        compiler_params=pltpu.CompilerParams(vmem_limit_bytes=16 * 2**20),
        name=name,
    )


def two_parts(x):
    high = x.astype(BF16).astype(F32)
    return jnp.concatenate([high, x - high], axis=0).astype(BF16)


def halves(x):
    high = x.astype(BF16)
    return high, (x - high.astype(F32)).astype(BF16)


def product(x, high, low, dims):
    parts = two_parts(x)
    both = lax.dot_general(parts, high, dims, preferred_element_type=F32)
    both = both + lax.dot_general(parts, low, dims, preferred_element_type=F32)
    rows = x.shape[0]
    return both[:rows] + both[rows:]


def offsets_of(columns, start):
    found = []
    for offset in range(1, 8):
        hit = jnp.int32(0)
        for slot in range(7):
            away = columns[0, slot] - start
            hit = hit | jnp.where((away == offset) | (away == -offset), 1, 0)
        found.append(hit * 16 + offset)
    first = functools.reduce(jnp.maximum, found)
    second = functools.reduce(jnp.maximum, [jnp.where(f == first, 0, f) for f in found])
    first, second = (first & 15, second & 15)
    return (jnp.minimum(first, second), jnp.maximum(first, second), jnp.int32(8))


def pack_kernel(rows_part, columns, tiles, pivots, own, part, offsets):
    shard_rows, slots, order, _ = tiles.shape
    start = (lax.axis_index("blk") * SPAN + lax.axis_index("pos")) * shard_rows
    offs = offsets_of(columns, start)
    for k in range(3):
        offsets[0, k] = offs[k]
    at = [lax.broadcasted_iota(jnp.int32, (order, order), d) for d in range(2)]
    for row in range(shard_rows):
        sums = [jnp.zeros((order, order), F32) for _ in range(4)]
        for slot in range(slots):
            away = columns[row, slot] - (start + row)
            tile = tiles[row, slot]
            for k, want in enumerate((*offs, 0)):
                sums[k] = sums[k] + tile * jnp.where(away == want, 1.0, 0.0)
        both = jnp.where(at[0] <= at[1], pivots[row], sums[3])
        line = jnp.sum(jnp.where(at[0] == at[1], sums[3], 0.0), axis=0, keepdims=True)
        own[row, :order] = jnp.concatenate([sums[0], sums[1]], axis=1)
        own[row, order : 2 * order] = jnp.concatenate([sums[2], both], axis=1)
        own[row, 2 * order :] = jnp.broadcast_to(jnp.concatenate([line, line], axis=1), (8, 2 * order))
    for r in range(rows_part):
        part[r] = own[lax.axis_index("rhs") * rows_part + r]


def band_kernel(columns, tiles, band_high, band_low, band):
    shard_rows, slots, order, _ = tiles.shape
    start = (lax.axis_index("blk") * SPAN + lax.axis_index("pos")) * shard_rows
    band[...] = jnp.zeros_like(band)
    for row in range(shard_rows):
        for slot in range(slots):
            away = columns[row, slot] - start + shard_rows
            where = pl.ds(pl.multiple_of(away * order, order), order)
            lanes = pl.ds(row * order, order)
            band[where, lanes] = band[where, lanes] + tiles[row, slot].T
    high, low = halves(band[...])
    band_high[...] = high
    band_low[...] = low


def stage_rows(stage, t, pieces):
    rows_part = pieces[0][0].shape[0]
    base = (lax.axis_index("rhs") ^ t) * rows_part
    for r in range(rows_part):
        top = 0
        for ref, first, rows in pieces:
            stage[base + r, top : top + rows] = ref[r, first : first + rows]
            top += rows


def factors(offsets, stages, groups, m_high, m_low, w_high, w_low, g_high, g_low):
    order = 64
    cells = 8 * order
    o = [offsets[0, k] for k in range(3)]
    at = [lax.broadcasted_iota(jnp.int32, (order, order), d) for d in range(2)]
    lane = lax.broadcasted_iota(jnp.int32, (order, 2 * order), 1)
    pivots = {}
    for n, (stage, s) in enumerate(zip(stages, groups)):
        for i in range(8):
            for k in range(3):
                from_row = (i - o[k]) & 7
                kind = jnp.where(o[k] > i, 0, 1)
                tile = stage[
                    from_row,
                    k // 2 * order : (k // 2 + 1) * order,
                    k % 2 * order : (k % 2 + 1) * order,
                ]
                high, low = halves(tile)
                where = pl.ds(pl.multiple_of(from_row * order, order), order)
                lanes = slice(i * order, (i + 1) * order)
                m_high[s, kind, where, lanes] = high
                m_low[s, kind, where, lanes] = low
            both = stage[i, order : 2 * order, order:]
            turned = both.T
            pivots[n, i] = jnp.where(at[0] <= at[1], both, turned)
            line = stage[i, 2 * order : 2 * order + 1, :order]
            tile = jnp.where(at[0] > at[1], both, jnp.where(at[0] < at[1], turned, line))
            high, low = halves(tile)
            where = slice(i % 2 * order, (i % 2 + 1) * order)
            g_high[s, i // 2, where, where] = high
            g_low[s, i // 2, where, where] = low
    lefts = {}
    for n, stage in enumerate(stages):
        for j in range(7):
            inside = [jnp.where(o[k] + j <= 7, 1.0, 0.0) for k in range(2)]
            pair = stage[j, :order] * jnp.where(lane < order, inside[0], inside[1])
            left = two_parts(product(pivots[n, j], *halves(pair), NN))
            lefts[n, j] = jnp.concatenate([left, left], axis=1)
    for j in range(7, -1, -1):
        for n, s in enumerate(groups):
            row = jnp.pad(pivots[n, j], ((0, 0), (j * order, cells - (j + 1) * order)))
            if j < 7:
                where = [
                    pl.ds(pl.multiple_of(jnp.minimum(o[k] + j, 7) * order, order), order)
                    for k in range(2)
                ]
                first = (j + 1) // 4 * 256
                right = jnp.concatenate(
                    [w[s, where[k], first:] for w in (w_high, w_low) for k in range(2)], axis=0
                )
                both = lax.dot_general(lefts[n, j], right, NN, preferred_element_type=F32)
                away = both[:order] + both[order:]
                if first:
                    away = jnp.pad(away, ((0, 0), (first, 0)))
                row = row - away
            high, low = halves(row)
            w_high[s, j * order : (j + 1) * order] = high
            w_low[s, j * order : (j + 1) * order] = low


def own_factor_kernel(offsets, own, m_high, m_low, w_high, w_low, g_high, g_low):
    for ref in (m_high, m_low, g_high, g_low):
        ref[...] = jnp.zeros_like(ref)
    mats = (m_high, m_low, w_high, w_low, g_high, g_low)
    factors(offsets, [own], [lax.axis_index("pos")], *mats)


def factor_kernel(layout, count, ins, mats, outs, scratch):
    offsets, given = ins[0], ins[1:]
    staged, groups = [], []
    for n, (mask, pieces) in enumerate(layout):
        stage = scratch[0].at[n]
        for t in range(count):
            stage_rows(stage, t, [(given[i * count + t], first, rows) for i, first, rows in pieces])
        staged.append(stage)
        groups.append(lax.axis_index("pos") ^ mask)
    factors(offsets, staged, groups, *mats)


def upper(x, high, low):
    half = high.shape[0] // 2
    return jnp.concatenate(
        [
            product(x[:, :half], high[:half, :half], low[:half, :half], NN),
            product(x, high[:, half:], low[:, half:], NN),
        ],
        axis=1,
    )


def upper_t(x, high, low):
    half = high.shape[0] // 2
    return jnp.concatenate(
        [
            product(x, high[:half], low[:half], NT),
            product(x[:, half:], high[half:, half:], low[half:, half:], NT),
        ],
        axis=1,
    )


def lower(x, high, low):
    half = high.shape[0] // 2
    return jnp.concatenate(
        [
            product(x, high[:, :half], low[:, :half], NN),
            product(x[:, half:], high[half:, half:], low[half:, half:], NN),
        ],
        axis=1,
    )


def lower_t(x, high, low):
    half = high.shape[0] // 2
    return jnp.concatenate(
        [
            product(x[:, :half], high[:half, :half], low[:half, :half], NT),
            product(x, high[half:], low[half:], NT),
        ],
        axis=1,
    )


def forward_step(s, source, before, m, w):
    if before is not None:
        source = source - lower(before, m[0].at[s - 1, 0], m[1].at[s - 1, 0])
    value = upper(source, w[0].at[s], w[1].at[s])
    return value, source - upper(value, m[0].at[s, 1], m[1].at[s, 1])


def first_kernel(mats, r, t, top):
    m, w = mats[:2], mats[2:4]
    value = None
    for s in range(8):
        value, t[s] = forward_step(s, r[s], value, m, w)
    z = upper_t(t[7], w[0][7], w[1][7])
    top[0] = z
    top[1] = lower(z, m[0][7, 0], m[1][7, 0])


def spread(out, values):
    zero = jnp.zeros_like(values[0])
    for s in range(8):
        for side in range(3):
            out[s, side] = values[s + side - 1] if 0 <= s + side - 1 < 8 else zero


def second_kernel(mats, t, top, z, above, out, ends):
    m, w = mats[:2], mats[2:4]
    value = top[0]
    values = {7: value}
    for s in range(6, -1, -1):
        above[s] = lower_t(value, m[0][s, 0], m[1][s, 0])
        value = upper_t(t[s] - above[s], w[0][s], w[1][s])
        values[s] = value
    above[7] = jnp.zeros_like(value)
    for s in range(8):
        z[s] = values[s]
    spread(out, values)
    ends[:2] = top[...]
    ends[2] = value


def third_kernel(mats, r, t, z, above, source, t_left):
    m, g = mats[:2], mats[4:]
    for s in range(8):
        x = z[s]
        ahead = upper_t(x, m[0][s, 1], m[1][s, 1]) + above[s]
        own = [
            product(x[:, i * 128 : (i + 1) * 128], g[0][s, i], g[1][s, i], NN) for i in range(4)
        ]
        t_left[s] = t[s] - ahead
        source[s] = jnp.concatenate(own, axis=1) + ahead - t_left[s] - r[s]


def fourth_kernel(mats, source, t_left, from_below, from_above, t, last):
    m, w = mats[:2], mats[2:4]
    before = None
    for s in range(8):
        start = source[s]
        if s == 0:
            start = start + from_below[1]
        if s == 7:
            start = start + lower_t(from_above[2], m[0][7, 0], m[1][7, 0])
        before, more = forward_step(s, start, before, m, w)
        t[s] = t_left[s] + more
    last[...] = upper_t(t[7], w[0][7], w[1][7])


def fifth_kernel(mats, t, last, out):
    m, w = mats[:2], mats[2:4]
    value = last[...]
    values = {7: value}
    for s in range(6, -1, -1):
        ahead = lower_t(value, m[0][s, 0], m[1][s, 0])
        value = upper_t(t[s] - ahead, w[0][s], w[1][s])
        values[s] = value
    spread(out, values)


def place_rows(place, t, rhs, rows, lanes=slice(None)):
    count = rows.shape[0]
    place[pl.ds(pl.multiple_of((rhs ^ t) * count, count), count), lanes] = rows


def image_of(pieces, wide, band_high, band_low):
    rhs, cells = lax.axis_index("rhs"), pieces[0].shape[3]
    for t, piece in enumerate(pieces):
        for side in range(3):
            rows = jnp.concatenate([piece[j, side] for j in range(SPAN)], axis=0)
            place_rows(wide, t, rhs, rows, slice(side * cells, (side + 1) * cells))
    below = product(wide[:, :cells], band_high[:cells], band_low[:cells], NN)
    image = below + product(wide[:, cells:], band_high[cells:], band_low[cells:], NN)
    twice = image + below * jnp.where(lax.axis_index("pos") == 0, 1.0, 0.0)
    return wide[:, cells : 2 * cells], image, twice


def inner(a, b):
    return lax.dot_general(a, b, NT, precision=HIGHEST, preferred_element_type=F32)


def early_kernel(n, *refs):
    r_pieces, pieces = refs[:n], refs[n : 2 * n]
    band_high, band_low, r, d, q, sums, wide = refs[2 * n :]
    for t in range(n):
        place_rows(r, t, lax.axis_index("rhs"), r_pieces[t][...])
    d[...], q[...], twice = image_of(pieces, wide, band_high, band_low)
    sums[0] = inner(d[...], r[...])
    sums[1] = inner(d[...], twice)


def late_kernel(n, *refs):
    pieces = refs[:n]
    q, band_high, band_low, e, w, sums, wide = refs[n:]
    e[...], w[...], twice = image_of(pieces, wide, band_high, band_low)
    sums[0] = inner(e[...], q[...])
    sums[1] = inner(e[...], twice)


def complete_kernel(value, arrived, band_high, band_low, out):
    cells = value.shape[1]
    above = slice(2 * cells, 3 * cells)
    out[...] = value[...] + product(arrived[...], band_high[above], band_low[above], NN)


def small(a, b):
    return lax.dot_general(a, b, NN, precision=HIGHEST, preferred_element_type=F32)


def inverse(a):
    size = a.shape[0]
    row_at = lax.broadcasted_iota(jnp.int32, a.shape, 0)
    col_at = lax.broadcasted_iota(jnp.int32, a.shape, 1)
    for k in range(size):
        scale = 1.0 / a[k : k + 1, k : k + 1]
        row = jnp.where(col_at[:1] == k, 1.0, a[k : k + 1, :]) * scale
        column = a[:, k : k + 1]
        rest = jnp.where(col_at == k, 0.0, a)
        a = jnp.where(row_at == k, row, rest - column * row)
    return a


def symmetric(a):
    return 0.5 * (a + a.T)


def invert_kernel(sums, inverted):
    inverted[...] = inverse(symmetric(sums[1]))


def last_kernel(early, late, inverted, r, d, q, e, w, solution, residual):
    count = solution.shape[0]
    rhs = lax.axis_index("rhs")
    s1, s2 = symmetric(early[0]), symmetric(early[1])
    s3, s4 = symmetric(late[0]), symmetric(late[1])
    inv = inverted[...]
    c = small(inv, s3)
    schur = symmetric(s4 - small(s3, c))
    h = small(s2 - s1 - small(s1, c), inverse(schur))
    f = small(s1 - small(h, s3), inv)
    pick = lax.broadcasted_iota(jnp.int32, (count, s1.shape[0]), 0) + rhs * count
    pick = jnp.where(pick == lax.broadcasted_iota(jnp.int32, pick.shape, 1), 1.0, 0.0)
    f, h = small(pick, f), small(pick, h)
    solution[...] = small(f, d[...]) + small(h, e[...])
    own = r[pl.ds(pl.multiple_of(rhs * count, count), count), :]
    residual[...] = own - small(f, q[...]) - small(h, w[...])


def swapped(value, axis, bit):
    return lax.ppermute(value, axis, [(i, i ^ bit) for i in range(lax.axis_size(axis))])


def summed(value):
    axes = ("blk", "pos")
    size = lax.axis_size(axes)
    bit = 1
    while bit < size:
        near = value + swapped(value, axes, bit)
        if 2 * bit < size:
            near = near + (swapped(value, axes, 2 * bit) + swapped(value, axes, 3 * bit))
        value = near
        bit *= 4
    return value


def both_ways(value):
    blocks = lax.axis_size("blk")
    low = high = None
    for first in range(min(2, blocks - 1)):
        pairs = [(i, i + 1) for i in range(first, blocks - 1, 2)]
        got = lax.ppermute(value, "blk", pairs + [(b, a) for a, b in pairs])
        even = lax.axis_index("blk") % 2 == first
        up, down = jnp.where(even, 0.0, got), jnp.where(even, got, 0.0)
        low, high = (up, down) if low is None else (low + up, high + down)
    return low, high


def shards(right_side, tiles, pivots, columns):
    count, cells = right_side.shape
    shard_rows, slots, order, _ = tiles.shape
    parts = lax.axis_size("rhs")
    blocks = lax.axis_size("blk")
    rows_part = shard_rows // parts
    each = count // SPAN
    total = count * parts
    S = jax.ShapeDtypeStruct
    up = [(i, i + 1) for i in range(blocks - 1)]
    down_rows = [(SPAN * (i + 1), SPAN * (i + 1) - 1) for i in range(blocks - 1)]

    def others(value):
        return [value] + [swapped(value, "rhs", t) for t in range(1, parts)]

    tall = 2 * order + 8
    own, part, offsets = call(
        functools.partial(pack_kernel, rows_part),
        "pack_tiles",
        [
            S((shard_rows, tall, 2 * order), F32),
            S((rows_part, tall, 2 * order), F32),
            S((1, 3), jnp.int32),
        ],
        [SMEM, VMEM, VMEM],
        [VMEM, VMEM, SMEM],
        cost=2,
    )(columns, tiles, pivots)

    x, y, z = (swapped(part, "pos", bit) for bit in (1, 2, 4))
    mat_shapes = [
        pltpu.VMEM((SPAN, 2, cells, cells), BF16),
        pltpu.VMEM((SPAN, 2, cells, cells), BF16),
        pltpu.VMEM((SPAN, cells, cells), BF16),
        pltpu.VMEM((SPAN, cells, cells), BF16),
        pltpu.VMEM((SPAN, 4, 2 * order, 2 * order), BF16),
        pltpu.VMEM((SPAN, 4, 2 * order, 2 * order), BF16),
    ]
    r = lax.all_to_all(right_side.reshape(SPAN, each, cells), "pos", 0, 0, tiled=True)
    own, r = lax.optimization_barrier((own, r))
    mats = call(own_factor_kernel, "factors_own", mat_shapes, [SMEM, VMEM], [VMEM] * 6, cost=4)(
        offsets, own
    )
    band_high, band_low = call(
        band_kernel,
        "row_band",
        [S((3 * cells, cells), BF16)] * 2,
        [SMEM, VMEM],
        [VMEM] * 2,
        [pltpu.VMEM((3 * cells, cells), F32)],
        cost=3,
    )(columns, tiles)

    def with_mats(kernel, name, specs, out_shapes, given, scratch=(), cost=1):
        nonlocal mats
        first, outs = len(given), len(out_shapes)

        def body(*refs):
            ins, rest = refs[:first], refs[first + 6 :]
            kernel(ins, rest[outs : outs + 6], rest[:outs], rest[outs + 6 :])

        *results, m0, m1, w0, w1, g0, g1 = call(
            body,
            name,
            [*out_shapes, *mat_shapes],
            [*specs, *[VMEM] * 6],
            [VMEM] * (outs + 6),
            scratch,
            {first + i: outs + i for i in range(6)},
            cost,
        )(*given, *mats)
        mats = [m0, m1, w0, w1, g0, g1]
        return results

    def add_factors(name, layout, operands, cost):
        given = [offsets] + [piece for operand in operands for piece in others(operand)]
        with_mats(
            functools.partial(factor_kernel, layout, parts),
            name,
            [SMEM] + [VMEM] * (len(given) - 1),
            [],
            given,
            [pltpu.VMEM((len(layout), shard_rows, tall, 2 * order), F32)],
            cost,
        )

    def sweep(kernel, name, out_shapes, *given, cost=1):
        def body(ins, held, outs, scratch):
            kernel(held, *ins, *outs)

        return with_mats(body, name, [VMEM] * len(given), out_shapes, given, cost=cost)

    join = lambda *pieces: jnp.concatenate(pieces, axis=1)
    xs = swapped(join(y[:, :order], z[:, :order]), "pos", 1)
    ys = swapped(join(x[:, order:], z[:, :order]), "pos", 2)
    zs = swapped(join(x[:, order:], y[:, order:]), "pos", 4)
    rest = tall - order
    far_top = swapped(ys[:, rest:], "pos", 1)
    far_low = swapped(ys[:, :rest], "pos", 4)
    add_factors(
        "factors_near", [(bit, [(i, 0, tall)]) for i, bit in enumerate((1, 2, 4))], [x, y, z], 6
    )
    add_factors(
        "factors_mid",
        [
            (3, [(0, 0, order), (1, 0, rest)]),
            (5, [(0, order, order), (2, 0, rest)]),
            (6, [(1, rest, order), (2, rest, rest)]),
        ],
        [xs, ys, zs],
        6,
    )
    add_factors("factors_far", [(7, [(0, 0, order), (1, 0, rest)])], [far_top, far_low], 3)

    r_pieces = others(right_side)
    vectors, vector = S((SPAN, each, cells), F32), S((each, cells), F32)
    ends_shape, spread_shape = S((3, each, cells), F32), S((SPAN, 3, each, cells), F32)
    t, top = sweep(first_kernel, "forward_r", [vectors, S((2, each, cells), F32)], r, cost=4)
    z, above, spread_z, ends = sweep(
        second_kernel, "backward_r", [vectors, vectors, spread_shape, ends_shape], t, top, cost=4
    )
    from_below, from_above = both_ways(ends)
    source, t_left = sweep(third_kernel, "residue_of_z", [vectors] * 2, r, t, z, above, cost=2)
    spread_z = (spread_z.at[0, 0].set(from_below[0]))
    t, last = sweep(
        fourth_kernel, "forward_v", [vectors, vector], source, t_left, from_below, from_above, cost=4
    )
    from_below = lax.ppermute(last, "blk", up)
    (spread_e,) = sweep(fifth_kernel, "backward_v", [spread_shape], t, last, cost=4)
    both = jnp.stack([spread_z, spread_e.at[0, 0].set(from_below)], axis=1)
    both = lax.all_to_all(both, "pos", 0, 0, tiled=True)
    spread_z, spread_e = both[:, 0], both[:, 1]

    full, two = S((total, cells), F32), S((2, total, total), F32)
    wide = pltpu.VMEM((total, 3 * cells), F32)
    r_full, d_full, q_part, early = call(
        functools.partial(early_kernel, parts),
        "products_d",
        [full, full, full, two],
        [VMEM] * (2 * parts + 2),
        [VMEM] * 4,
        [wide],
    )(*r_pieces, *others(spread_z), band_high, band_low)
    d_above = lax.ppermute(d_full, ("blk", "pos"), down_rows)
    early = summed(early)
    inverted = call(invert_kernel, "invert", S((total, total), F32), [VMEM])(early)
    complete = call(complete_kernel, "complete", full, [VMEM] * 4)
    q_full = complete(q_part, d_above, band_high, band_low)

    e_full, w_part, late = call(
        functools.partial(late_kernel, parts),
        "products_e",
        [full, full, two],
        [VMEM] * (parts + 3),
        [VMEM] * 3,
        [wide],
    )(*others(spread_e), q_full, band_high, band_low)
    late = summed(late)
    e_above = lax.ppermute(e_full, ("blk", "pos"), down_rows)
    w_full = complete(w_part, e_above, band_high, band_low)
    return call(
        last_kernel, "update", [S((count, cells), F32)] * 2, [VMEM] * 8, [VMEM] * 2
    )(early, late, inverted, r_full, d_full, q_full, e_full, w_full)


def solution(mesh):
    devices = mesh.devices
    split = Mesh(
        devices.reshape(devices.shape[0] // SPAN, SPAN, devices.shape[1]), ("blk", "pos", "rhs")
    )
    rows = ("blk", "pos")
    return jax.shard_map(
        shards,
        mesh=split,
        in_specs=(
            P("rhs", rows),
            P(rows, None, None, None),
            P(rows, None, None),
            P(rows, None),
        ),
        out_specs=(P("rhs", rows), P("rhs", rows)),
        check_vma=False,
    )
```

```python
import functools
import jax
import jax.numpy as jnp
from jax import lax
from jax.experimental import pallas as pl
from jax.experimental.pallas import tpu as pltpu
from jax.sharding import Mesh, PartitionSpec as P

SPAN = 8
F32 = jnp.float32
BF16 = jnp.bfloat16
HIGHEST = lax.Precision.HIGHEST
NN = (((1,), (0,)), ((), ()))
NT = (((1,), (1,)), ((), ()))
VMEM = pl.BlockSpec(memory_space=pltpu.VMEM)
SMEM = pl.BlockSpec(memory_space=pltpu.SMEM)


def call(kernel, name, out_shape, in_specs, out_specs=VMEM, scratch=(), aliases=None, cost=1):
    return pl.pallas_call(
        kernel,
        out_shape=out_shape,
        in_specs=in_specs,
        out_specs=out_specs,
        scratch_shapes=list(scratch),
        input_output_aliases=aliases or {},
        cost_estimate=pl.CostEstimate(flops=int(cost * 1e9), bytes_accessed=0, transcendentals=0),
        compiler_params=pltpu.CompilerParams(vmem_limit_bytes=16 * 2**20),
        name=name,
    )


def two_parts(x):
    high = x.astype(BF16).astype(F32)
    return jnp.concatenate([high, x - high], axis=0).astype(BF16)


def halves(x):
    high = x.astype(BF16)
    return high, (x - high.astype(F32)).astype(BF16)


def product(x, high, low, dims):
    parts = two_parts(x)
    both = lax.dot_general(parts, high, dims, preferred_element_type=F32)
    both = both + lax.dot_general(parts, low, dims, preferred_element_type=F32)
    rows = x.shape[0]
    return both[:rows] + both[rows:]


def offsets_of(columns, start):
    found = []
    for offset in range(1, 8):
        hit = jnp.int32(0)
        for slot in range(7):
            away = columns[0, slot] - start
            hit = hit | jnp.where((away == offset) | (away == -offset), 1, 0)
        found.append(hit * 16 + offset)
    first = functools.reduce(jnp.maximum, found)
    second = functools.reduce(jnp.maximum, [jnp.where(f == first, 0, f) for f in found])
    first, second = (first & 15, second & 15)
    return (jnp.minimum(first, second), jnp.maximum(first, second), jnp.int32(8))


def pack_kernel(rows_part, columns, tiles, pivots, own, part, offsets):
    shard_rows, slots, order, _ = tiles.shape
    start = (lax.axis_index("blk") * SPAN + lax.axis_index("pos")) * shard_rows
    offs = offsets_of(columns, start)
    for k in range(3):
        offsets[0, k] = offs[k]
    at = [lax.broadcasted_iota(jnp.int32, (order, order), d) for d in range(2)]
    for row in range(shard_rows):
        sums = [jnp.zeros((order, order), F32) for _ in range(4)]
        for slot in range(slots):
            away = columns[row, slot] - (start + row)
            tile = tiles[row, slot]
            for k, want in enumerate((*offs, 0)):
                sums[k] = sums[k] + tile * jnp.where(away == want, 1.0, 0.0)
        both = jnp.where(at[0] <= at[1], pivots[row], sums[3])
        line = jnp.sum(jnp.where(at[0] == at[1], sums[3], 0.0), axis=0, keepdims=True)
        own[row, :order] = jnp.concatenate([sums[0], sums[1]], axis=1)
        own[row, order : 2 * order] = jnp.concatenate([sums[2], both], axis=1)
        own[row, 2 * order :] = jnp.broadcast_to(jnp.concatenate([line, line], axis=1), (8, 2 * order))
    for r in range(rows_part):
        part[r] = own[lax.axis_index("rhs") * rows_part + r]


def band_kernel(first_row, columns, tiles, band_high, band_low, band):
    shard_rows, slots, order, _ = tiles.shape
    start = (lax.axis_index("blk") * SPAN + lax.axis_index("pos")) * shard_rows
    band[...] = jnp.zeros_like(band)
    for row in range(shard_rows // 2):
        for slot in range(slots):
            away = columns[first_row + row, slot] - start + shard_rows
            where = pl.ds(pl.multiple_of(away * order, order), order)
            lanes = pl.ds(row * order, order)
            band[where, lanes] = band[where, lanes] + tiles[first_row + row, slot].T
    high, low = halves(band[...])
    band_high[...] = high
    band_low[...] = low


def along(x, bands, first, last):
    return jnp.concatenate(
        [product(x, high[first:last], low[first:last], NN) for high, low in zip(bands[::2], bands[1::2])],
        axis=1,
    )


def stage_rows(stage, t, pieces):
    rows_part = pieces[0][0].shape[0]
    base = (lax.axis_index("rhs") ^ t) * rows_part
    for r in range(rows_part):
        top = 0
        for ref, first, rows in pieces:
            stage[base + r, top : top + rows] = ref[r, first : first + rows]
            top += rows


def factors(offsets, stages, split, groups, m_high, m_low, w_high, w_low, g_high, g_low):
    order = 64
    o = [offsets[0, k] for k in range(3)]
    at = [lax.broadcasted_iota(jnp.int32, (order, order), d) for d in range(2)]
    lane = lax.broadcasted_iota(jnp.int32, (order, 2 * order), 1)
    pivots, lefts = {}, {}
    for n, (stage, s) in enumerate(zip(stages, groups)):
        for i in range(8):
            for p in range(2):
                pair = stage[i, p * order : (p + 1) * order]
                turned = jnp.concatenate([pair[:, order:], pair[:, :order]], axis=1)
                for version, tiles in enumerate((pair, turned)):
                    split[n, 0, i, version, p], split[n, 1, i, version, p] = halves(tiles)
            both = stage[i, order : 2 * order, order:]
            turned = both.T
            pivots[n, i] = jnp.where(at[0] <= at[1], both, turned)
            line = stage[i, 2 * order : 2 * order + 1, :order]
            tile = jnp.where(at[0] > at[1], both, jnp.where(at[0] < at[1], turned, line))
            high, low = halves(tile)
            where = slice(i % 2 * order, (i % 2 + 1) * order)
            g_high[s, i // 2, where, where] = high
            g_low[s, i // 2, where, where] = low
        for j in range(7):
            inside = [jnp.where(o[k] + j <= 7, 1.0, 0.0) for k in range(2)]
            pair = stage[j, :order] * jnp.where(lane < order, inside[0], inside[1])
            left = two_parts(product(pivots[n, j], *halves(pair), NN))
            lefts[n, j] = jnp.concatenate([left, left], axis=1)
        for i in range(8):
            lanes = slice(i * order, (i + 1) * order)
            side = slice(i % 2 * order, (i % 2 + 1) * order)
            for k in range(3):
                from_row = (i - o[k]) & 7 if k < 2 else i
                kind = jnp.where(o[k] > i, 0, 1) if k < 2 else 0
                where = pl.ds(pl.multiple_of(from_row * order, order), order)
                for part, m in enumerate((m_high, m_low)):
                    m[s, kind, where, lanes] = split[n, part, from_row, (i + k) % 2, k // 2, :, side]
    for j in range(7, -1, -1):
        first = j // 2 * 128
        for n, s in enumerate(groups):
            after = 8 * order - first - (j % 2 + 1) * order
            row = jnp.pad(pivots[n, j], ((0, 0), (j % 2 * order, after)))
            if j < 7:
                where = [
                    pl.ds(pl.multiple_of(jnp.minimum(o[k] + j, 7) * order, order), order)
                    for k in range(2)
                ]
                right = jnp.concatenate(
                    [w[s, where[k], first:] for w in (w_high, w_low) for k in range(2)], axis=0
                )
                both = lax.dot_general(lefts[n, j], right, NN, preferred_element_type=F32)
                row = row - (both[:order] + both[order:])
            high, low = halves(row)
            w_high[s, j * order : (j + 1) * order, first:] = high
            w_low[s, j * order : (j + 1) * order, first:] = low


def own_factor_kernel(offsets, own, m_high, m_low, w_high, w_low, g_high, g_low, split):
    mats = (m_high, m_low, w_high, w_low, g_high, g_low)
    for ref in mats:
        ref[...] = jnp.zeros_like(ref)
    factors(offsets, [own], split, [lax.axis_index("pos")], *mats)


def factor_kernel(layout, count, ins, mats, outs, scratch):
    offsets, given = ins[0], ins[1:]
    staged, groups = [], []
    for n, (mask, pieces) in enumerate(layout):
        stage = scratch[0].at[n]
        for t in range(count):
            stage_rows(stage, t, [(given[i * count + t], first, rows) for i, first, rows in pieces])
        staged.append(stage)
        groups.append(lax.axis_index("pos") ^ mask)
    factors(offsets, staged, scratch[1], groups, *mats)


def upper(x, high, low):
    half = high.shape[0] // 2
    return jnp.concatenate(
        [
            product(x[:, :half], high[:half, :half], low[:half, :half], NN),
            product(x, high[:, half:], low[:, half:], NN),
        ],
        axis=1,
    )


def upper_t(x, high, low):
    half = high.shape[0] // 2
    return jnp.concatenate(
        [
            product(x, high[:half], low[:half], NT),
            product(x[:, half:], high[half:, half:], low[half:, half:], NT),
        ],
        axis=1,
    )


def lower(x, high, low):
    half = high.shape[0] // 2
    return jnp.concatenate(
        [
            product(x, high[:, :half], low[:, :half], NN),
            product(x[:, half:], high[half:, half:], low[half:, half:], NN),
        ],
        axis=1,
    )


def lower_t(x, high, low):
    half = high.shape[0] // 2
    return jnp.concatenate(
        [
            product(x[:, :half], high[:half, :half], low[:half, :half], NT),
            product(x, high[half:], low[half:], NT),
        ],
        axis=1,
    )


def forward_step(s, source, before, m, w):
    if before is not None:
        source = source - lower(before, m[0].at[s - 1, 0], m[1].at[s - 1, 0])
    value = upper(source, w[0].at[s], w[1].at[s])
    return value, source - upper(value, m[0].at[s, 1], m[1].at[s, 1])


def first_kernel(mats, r, t, top):
    m, w = mats[:2], mats[2:4]
    value = None
    for s in range(8):
        value, t[s] = forward_step(s, r[s], value, m, w)
    z = upper_t(t[7], w[0][7], w[1][7])
    top[0] = z
    top[1] = lower(z, m[0][7, 0], m[1][7, 0])


def spread(out, kind, values, below, above):
    values = [below, *values, above]
    for s in range(8):
        for side in range(3):
            out[s, kind, side] = values[s + side]


def second_kernel(mats, t, top, z, above, ends):
    m, w = mats[:2], mats[2:4]
    value = top[0]
    values = {7: value}
    for s in range(6, -1, -1):
        above[s] = lower_t(value, m[0][s, 0], m[1][s, 0])
        value = upper_t(t[s] - above[s], w[0][s], w[1][s])
        values[s] = value
    above[7] = jnp.zeros_like(value)
    for s in range(8):
        z[s] = values[s]
    ends[:2] = top[...]
    ends[2] = value


def third_kernel(mats, r, t, z, above, source, t_left):
    m, g = mats[:2], mats[4:]
    for s in range(8):
        x = z[s]
        ahead = upper_t(x, m[0][s, 1], m[1][s, 1]) + above[s]
        own = [
            product(x[:, i * 128 : (i + 1) * 128], g[0][s, i], g[1][s, i], NN) for i in range(4)
        ]
        t_left[s] = t[s] - ahead
        source[s] = jnp.concatenate(own, axis=1) + ahead - t_left[s] - r[s]


def fourth_kernel(mats, source, t_left, from_below, from_above, t, last):
    m, w = mats[:2], mats[2:4]
    before = None
    for s in range(8):
        start = source[s]
        if s == 0:
            start = start + from_below[1]
        if s == 7:
            start = start + lower_t(from_above[2], m[0][7, 0], m[1][7, 0])
        before, more = forward_step(s, start, before, m, w)
        t[s] = t_left[s] + more
    last[...] = upper_t(t[7], w[0][7], w[1][7])


def fifth_kernel(mats, t, last, z, from_below, from_above, out):
    m, w = mats[:2], mats[2:4]
    value = last[...]
    values = [value]
    for s in range(6, -1, -1):
        ahead = lower_t(value, m[0][s, 0], m[1][s, 0])
        value = upper_t(t[s] - ahead, w[0][s], w[1][s])
        values.insert(0, value)
    zero = jnp.zeros_like(value)
    spread(out, 0, [z[s] for s in range(8)], from_below[0], from_above[2])
    spread(out, 1, values, zero, zero)


def halo_kernel(rows, arrived, out):
    out[0, 1, 0] = arrived[...]


def place_rows(place, t, rhs, rows, lanes=slice(None)):
    count = rows.shape[0]
    place[pl.ds(pl.multiple_of((rhs ^ t) * count, count), count), lanes] = rows


def inner(a, b):
    return lax.dot_general(a, b, NT, precision=HIGHEST, preferred_element_type=F32)


def products_kernel(n, *refs):
    r_pieces, pieces, bands = refs[:n], refs[n : 2 * n], refs[2 * n : 2 * n + 4]
    r, d, q, e, w, sums, wide = refs[2 * n + 4 :]
    rhs, cells, total = lax.axis_index("rhs"), pieces[0].shape[4], r.shape[0]
    for t in range(n):
        place_rows(r, t, rhs, r_pieces[t][...])
        for kind in range(2):
            for side in range(3):
                rows = jnp.concatenate([pieces[t][j, kind, side] for j in range(SPAN)], axis=0)
                lanes = slice(side * cells, (side + 1) * cells)
                place_rows(wide.at[pl.ds(kind * total, total)], t, rhs, rows, lanes)
    below = along(wide[:, :cells], bands, 0, cells)
    image = below + along(wide[:, cells:], bands, cells, 3 * cells)
    first = jnp.where(lax.axis_index("pos") == 0, 1.0, 0.0)
    below_e = below[total:] * first
    own = slice(cells, 2 * cells)
    d[...], e[...] = wide[:total, own], wide[total:, own]
    q[...], w[...] = image[:total], image[total:]
    odd = rhs % 2 == 1
    left = jnp.where(odd, e[...], d[...])
    rights = jnp.where(odd, q[...], r[...]), jnp.where(odd, w[...] + below_e, q[...])
    sums[...] = jnp.concatenate([inner(left, right) for right in rights], axis=1)


def complete_kernel(value, arrived, *refs):
    cells = value.shape[1]
    refs[4][...] = value[...] + along(arrived[...], refs[:4], 2 * cells, 3 * cells)


def small(a, b):
    return lax.dot_general(a, b, NN, precision=HIGHEST, preferred_element_type=F32)


def inverse(a):
    at = [lax.broadcasted_iota(jnp.int32, a.shape, d) for d in range(2)]
    same = at[0] == at[1]
    eye = jnp.where(same, 1.0, 0.0)
    kept = jnp.where(same, a, 0.0)
    by_row = lax.rsqrt(jnp.sum(kept, axis=1, keepdims=True))
    by_column = lax.rsqrt(jnp.sum(kept, axis=0, keepdims=True))
    a = a * by_row * by_column
    scale = 1.0 / jnp.max(jnp.sum(jnp.abs(a), axis=0, keepdims=True), axis=1, keepdims=True)
    rest = eye - a * scale
    total = eye + rest

    def step(total, rest):
        rest = product(rest, *halves(rest), NN)
        return total + product(total, *halves(rest), NN), rest

    for _ in range(5):
        total, rest = step(total, rest)

    def going(carry):
        turn, _, rest = carry
        return (turn < 40) & (jnp.max(jnp.abs(rest)) > 1e-7)

    def more(carry):
        turn, total, rest = carry
        return (turn + 1, *step(total, rest))

    _, total, _ = lax.while_loop(going, more, (jnp.int32(0), total, rest))
    total = total * scale
    total = total + small(total, eye - small(a, total))
    return total * by_row * by_column


def symmetric(a):
    return 0.5 * (a + a.T)


def last_kernel(own_sums, other_sums, r, d, q, e, w, solution, residual):
    count, total = solution.shape[0], r.shape[0]
    rhs = lax.axis_index("rhs")
    odd = rhs % 2 == 1
    sums = jnp.where(odd, other_sums[...], own_sums[...]), jnp.where(odd, own_sums[...], other_sums[...])
    s1, s2, s3, s4 = [
        symmetric(sums[k // 2][:, k % 2 * total : (k % 2 + 1) * total]) for k in range(4)
    ]
    inv = inverse(s2)
    c = small(inv, s3)
    schur = symmetric(s4 - small(s3, c))
    h = small(s2 - s1 - small(s1, c), inverse(schur))
    f = small(s1 - small(h, s3), inv)
    pick = lax.broadcasted_iota(jnp.int32, (count, total), 0) + rhs * count
    pick = jnp.where(pick == lax.broadcasted_iota(jnp.int32, pick.shape, 1), 1.0, 0.0)
    f, h = small(pick, f), small(pick, h)
    solution[...] = small(f, d[...]) + small(h, e[...])
    own = r[pl.ds(pl.multiple_of(rhs * count, count), count), :]
    residual[...] = own - small(f, q[...]) - small(h, w[...])


def swapped(value, axis, bit):
    return lax.ppermute(value, axis, [(i, i ^ bit) for i in range(lax.axis_size(axis))])


def summed(value):
    axes = ("blk", "pos")
    size = lax.axis_size(axes)
    bit = 1
    while bit < size:
        near = value + swapped(value, axes, bit)
        if 2 * bit < size:
            near = near + (swapped(value, axes, 2 * bit) + swapped(value, axes, 3 * bit))
        value = near
        bit *= 4
    return value


def both_ways(value):
    blocks = lax.axis_size("blk")
    low = high = None
    for first in range(min(2, blocks - 1)):
        pairs = [(i, i + 1) for i in range(first, blocks - 1, 2)]
        got = lax.ppermute(value, "blk", pairs + [(b, a) for a, b in pairs])
        even = lax.axis_index("blk") % 2 == first
        up, down = jnp.where(even, 0.0, got), jnp.where(even, got, 0.0)
        low, high = (up, down) if low is None else (low + up, high + down)
    return low, high


def shards(right_side, tiles, pivots, columns):
    count, cells = right_side.shape
    shard_rows, slots, order, _ = tiles.shape
    parts = lax.axis_size("rhs")
    blocks = lax.axis_size("blk")
    rows_part = shard_rows // parts
    each = count // SPAN
    total = count * parts
    S = jax.ShapeDtypeStruct
    up = [(i, i + 1) for i in range(blocks - 1)]
    down_rows = [(SPAN * (i + 1), SPAN * (i + 1) - 1) for i in range(blocks - 1)]

    def others(value):
        return [value] + [swapped(value, "rhs", t) for t in range(1, parts)]

    tall = 2 * order + 8
    own, part, offsets = call(
        functools.partial(pack_kernel, rows_part),
        "pack_tiles",
        [
            S((shard_rows, tall, 2 * order), F32),
            S((rows_part, tall, 2 * order), F32),
            S((1, 3), jnp.int32),
        ],
        [SMEM, VMEM, VMEM],
        [VMEM, VMEM, SMEM],
        cost=2,
    )(columns, tiles, pivots)

    vectors, vector = S((SPAN, each, cells), F32), S((each, cells), F32)
    r = lax.all_to_all(right_side.reshape(SPAN, each, cells), "pos", 0, 0, tiled=True)
    x, y, z = (swapped(part, "pos", bit) for bit in (1, 2, 4))
    mat_shapes = [
        pltpu.VMEM((SPAN, 2, cells, cells), BF16),
        pltpu.VMEM((SPAN, 2, cells, cells), BF16),
        pltpu.VMEM((SPAN, cells, cells), BF16),
        pltpu.VMEM((SPAN, cells, cells), BF16),
        pltpu.VMEM((SPAN, 4, 2 * order, 2 * order), BF16),
        pltpu.VMEM((SPAN, 4, 2 * order, 2 * order), BF16),
    ]
    splits = lambda groups: pltpu.VMEM((groups, 2, 8, 2, 2, order, 2 * order), BF16)
    bands = []
    for half in range(2):
        bands += call(
            functools.partial(band_kernel, half * shard_rows // 2),
            "row_band",
            [S((3 * cells, cells // 2), BF16)] * 2,
            [SMEM, VMEM],
            [VMEM] * 2,
            [pltpu.VMEM((3 * cells, cells // 2), F32)],
            cost=2,
        )(columns, tiles)

    own, r = lax.optimization_barrier((own, r))
    mats = call(
        own_factor_kernel,
        "factors_own",
        mat_shapes,
        [SMEM, VMEM],
        [VMEM] * 6,
        [splits(1)],
        cost=4,
    )(offsets, own)
    def with_mats(kernel, name, specs, out_shapes, given, scratch=(), cost=1):
        nonlocal mats
        first, outs = len(given), len(out_shapes)

        def body(*refs):
            ins, rest = refs[:first], refs[first + 6 :]
            kernel(ins, rest[outs : outs + 6], rest[:outs], rest[outs + 6 :])

        *results, m0, m1, w0, w1, g0, g1 = call(
            body,
            name,
            [*out_shapes, *mat_shapes],
            [*specs, *[VMEM] * 6],
            [VMEM] * (outs + 6),
            scratch,
            {first + i: outs + i for i in range(6)},
            cost,
        )(*given, *mats)
        mats = [m0, m1, w0, w1, g0, g1]
        return results

    def add_factors(name, layout, operands, cost):
        given = [offsets] + [piece for operand in operands for piece in others(operand)]
        with_mats(
            functools.partial(factor_kernel, layout, parts),
            name,
            [SMEM] + [VMEM] * (len(given) - 1),
            [],
            given,
            [pltpu.VMEM((len(layout), shard_rows, tall, 2 * order), F32), splits(len(layout))],
            cost,
        )

    def sweep(kernel, name, out_shapes, *given, cost=1):
        def body(ins, held, outs, scratch):
            kernel(held, *ins, *outs)

        return with_mats(body, name, [VMEM] * len(given), out_shapes, given, cost=cost)

    join = lambda *pieces: jnp.concatenate(pieces, axis=1)
    xs = swapped(join(y[:, :order], z[:, :order]), "pos", 1)
    ys = swapped(join(x[:, order:], z[:, :order]), "pos", 2)
    zs = swapped(join(x[:, order:], y[:, order:]), "pos", 4)
    rest = tall - order
    far_top = swapped(ys[:, rest:], "pos", 1)
    far_low = swapped(ys[:, :rest], "pos", 4)
    add_factors(
        "factors_near", [(bit, [(i, 0, tall)]) for i, bit in enumerate((1, 2, 4))], [x, y, z], 6
    )
    add_factors(
        "factors_mid",
        [
            (3, [(0, 0, order), (1, 0, rest)]),
            (5, [(0, order, order), (2, 0, rest)]),
            (6, [(1, rest, order), (2, rest, rest)]),
        ],
        [xs, ys, zs],
        6,
    )
    add_factors("factors_far", [(7, [(0, 0, order), (1, 0, rest)])], [far_top, far_low], 3)

    r_pieces = others(right_side)
    ends_shape, spread_shape = S((3, each, cells), F32), S((SPAN, 2, 3, each, cells), F32)
    t, top = sweep(first_kernel, "forward_r", [vectors, S((2, each, cells), F32)], r, cost=4)
    z, above, ends = sweep(
        second_kernel, "backward_r", [vectors, vectors, ends_shape], t, top, cost=4
    )
    from_below, from_above = both_ways(ends)
    source, t_left = sweep(third_kernel, "residue_of_z", [vectors] * 2, r, t, z, above, cost=2)
    t, last = sweep(
        fourth_kernel, "forward_v", [vectors, vector], source, t_left, from_below, from_above, cost=4
    )
    last_below = lax.ppermute(last, "blk", up)
    (rows,) = sweep(
        fifth_kernel, "backward_v", [spread_shape], t, last, z, from_below, from_above, cost=4
    )
    rows = call(halo_kernel, "halo", spread_shape, [VMEM] * 2, aliases={0: 0})(rows, last_below)
    rows = lax.all_to_all(rows, "pos", 0, 0, tiled=True)

    full, sums_shape = S((total, cells), F32), S((total, 2 * total), F32)
    r_full, d, q, e, w_part, sums = call(
        functools.partial(products_kernel, parts),
        "products",
        [full] * 5 + [sums_shape],
        [VMEM] * (2 * parts + 4),
        [VMEM] * 6,
        [pltpu.VMEM((2 * total, 3 * cells), F32)],
        cost=2,
    )(*r_pieces, *others(rows), *bands)
    sums = summed(sums)
    e_above = lax.ppermute(e, ("blk", "pos"), down_rows)
    w = call(complete_kernel, "complete", full, [VMEM] * 6)(w_part, e_above, *bands)
    return call(last_kernel, "update", [S((count, cells), F32)] * 2, [VMEM] * 7, [VMEM] * 2, cost=8)(
        sums, swapped(sums, "rhs", 1), r_full, d, q, e, w
    )


def solution(mesh):
    devices = mesh.devices
    split = Mesh(
        devices.reshape(devices.shape[0] // SPAN, SPAN, devices.shape[1]), ("blk", "pos", "rhs")
    )
    rows = ("blk", "pos")
    return jax.shard_map(
        shards,
        mesh=split,
        in_specs=(
            P("rhs", rows),
            P(rows, None, None, None),
            P(rows, None, None),
            P(rows, None),
        ),
        out_specs=(P("rhs", rows), P("rhs", rows)),
        check_vma=False,
    )
```

```python
import functools
import jax
import jax.numpy as jnp
from jax import lax
from jax.experimental import pallas as pl
from jax.experimental.pallas import tpu as pltpu
from jax.sharding import Mesh, PartitionSpec as P

SPAN = 8
F32 = jnp.float32
BF16 = jnp.bfloat16
HIGHEST = lax.Precision.HIGHEST
NN = (((1,), (0,)), ((), ()))
NT = (((1,), (1,)), ((), ()))
VMEM = pl.BlockSpec(memory_space=pltpu.VMEM)
SMEM = pl.BlockSpec(memory_space=pltpu.SMEM)


def call(kernel, name, out_shape, in_specs, out_specs=VMEM, scratch=(), aliases=None, cost=1, limit=16):
    return pl.pallas_call(
        kernel,
        out_shape=out_shape,
        in_specs=in_specs,
        out_specs=out_specs,
        scratch_shapes=list(scratch),
        input_output_aliases=aliases or {},
        cost_estimate=pl.CostEstimate(flops=int(cost * 1e9), bytes_accessed=0, transcendentals=0),
        compiler_params=pltpu.CompilerParams(vmem_limit_bytes=limit * 2**20),
        name=name,
    )


def two_parts(x):
    high = x.astype(BF16).astype(F32)
    return jnp.concatenate([high, x - high], axis=0).astype(BF16)


def halves(x):
    high = x.astype(BF16)
    return high, (x - high.astype(F32)).astype(BF16)


def product(x, high, low, dims):
    parts = two_parts(x)
    both = lax.dot_general(parts, high, dims, preferred_element_type=F32)
    both = both + lax.dot_general(parts, low, dims, preferred_element_type=F32)
    rows = x.shape[0]
    return both[:rows] + both[rows:]


def offsets_of(columns, start):
    found = []
    for offset in range(1, 8):
        hit = jnp.int32(0)
        for slot in range(7):
            away = columns[0, slot] - start
            hit = hit | jnp.where((away == offset) | (away == -offset), 1, 0)
        found.append(hit * 16 + offset)
    first = functools.reduce(jnp.maximum, found)
    second = functools.reduce(jnp.maximum, [jnp.where(f == first, 0, f) for f in found])
    first, second = (first & 15, second & 15)
    return (jnp.minimum(first, second), jnp.maximum(first, second), jnp.int32(8))


def pack_kernel(rows_part, columns_far, tiles_far, pivots_far, own, part, offsets, *scratch):
    columns, tiles, pivots, sems = scratch
    shard_rows, slots, order, _ = tiles.shape
    copies = [
        pltpu.make_async_copy(far, near, sems.at[i])
        for i, (far, near) in enumerate(((columns_far, columns), (pivots_far, pivots)))
    ]
    for row in range(shard_rows):
        copies.append(pltpu.make_async_copy(tiles_far.at[row], tiles.at[row], sems.at[2 + row]))
    for copy in copies:
        copy.start()
    copies[0].wait()
    start = (lax.axis_index("blk") * SPAN + lax.axis_index("pos")) * shard_rows
    offs = offsets_of(columns, start)
    for k in range(3):
        offsets[0, k] = offs[k]
    at = [lax.broadcasted_iota(jnp.int32, (order, order), d) for d in range(2)]
    copies[1].wait()
    for row in range(shard_rows):
        copies[2 + row].wait()
        sums = [jnp.zeros((order, order), F32) for _ in range(4)]
        for slot in range(slots):
            away = columns[row, slot] - (start + row)
            tile = tiles[row, slot]
            for k, want in enumerate((*offs, 0)):
                sums[k] = sums[k] + tile * jnp.where(away == want, 1.0, 0.0)
        both = jnp.where(at[0] <= at[1], pivots[row], sums[3])
        line = jnp.sum(jnp.where(at[0] == at[1], sums[3], 0.0), axis=0, keepdims=True)
        own[row, :order] = jnp.concatenate([sums[0], sums[1]], axis=1)
        own[row, order : 2 * order] = jnp.concatenate([sums[2], both], axis=1)
        own[row, 2 * order :] = jnp.broadcast_to(jnp.concatenate([line, line], axis=1), (8, 2 * order))
    for a in range(rows_part):
        part[a] = own[lax.axis_index("rhs") * rows_part + a]


def band_kernel(first_row, columns, tiles, band_high, band_low, band):
    shard_rows, slots, order, _ = tiles.shape
    start = (lax.axis_index("blk") * SPAN + lax.axis_index("pos")) * shard_rows
    band[...] = jnp.zeros_like(band)
    for row in range(shard_rows // 2):
        for slot in range(slots):
            away = columns[first_row + row, slot] - start + shard_rows
            where = pl.ds(pl.multiple_of(away * order, order), order)
            lanes = pl.ds(row * order, order)
            band[where, lanes] = band[where, lanes] + tiles[first_row + row, slot].T
    high, low = halves(band[...])
    band_high[...] = high
    band_low[...] = low


def along(x, bands, first, last):
    return jnp.concatenate(
        [product(x, high[first:last], low[first:last], NN) for high, low in zip(bands[::2], bands[1::2])],
        axis=1,
    )


def stage_rows(stage, t, pieces):
    rows_part = pieces[0][0].shape[0]
    base = (lax.axis_index("rhs") ^ t) * rows_part
    for r in range(rows_part):
        top = 0
        for ref, first, rows in pieces:
            stage[base + r, top : top + rows] = ref[r, first : first + rows]
            top += rows


def factors(offsets, stages, split, groups, m_high, m_low, w_high, w_low, g_high, g_low):
    order = 64
    o = [offsets[0, k] for k in range(3)]
    at = [lax.broadcasted_iota(jnp.int32, (order, order), d) for d in range(2)]
    lane = lax.broadcasted_iota(jnp.int32, (order, 2 * order), 1)
    pivots, lefts = {}, {}
    for n, (stage, s) in enumerate(zip(stages, groups)):
        for i in range(8):
            for p in range(2):
                pair = stage[i, p * order : (p + 1) * order]
                turned = jnp.concatenate([pair[:, order:], pair[:, :order]], axis=1)
                for version, tiles in enumerate((pair, turned)):
                    split[n, 0, i, version, p], split[n, 1, i, version, p] = halves(tiles)
            both = stage[i, order : 2 * order, order:]
            turned = both.T
            pivots[n, i] = jnp.where(at[0] <= at[1], both, turned)
            line = stage[i, 2 * order : 2 * order + 1, :order]
            tile = jnp.where(at[0] > at[1], both, jnp.where(at[0] < at[1], turned, line))
            high, low = halves(tile)
            where = slice(i % 2 * order, (i % 2 + 1) * order)
            g_high[s, i // 2, where, where] = high
            g_low[s, i // 2, where, where] = low
        for j in range(7):
            inside = [jnp.where(o[k] + j <= 7, 1.0, 0.0) for k in range(2)]
            pair = stage[j, :order] * jnp.where(lane < order, inside[0], inside[1])
            left = two_parts(product(pivots[n, j], *halves(pair), NN))
            lefts[n, j] = jnp.concatenate([left, left], axis=1)
        for i in range(8):
            lanes = slice(i * order, (i + 1) * order)
            side = slice(i % 2 * order, (i % 2 + 1) * order)
            for k in range(3):
                from_row = (i - o[k]) & 7 if k < 2 else i
                kind = jnp.where(o[k] > i, 0, 1) if k < 2 else 0
                where = pl.ds(pl.multiple_of(from_row * order, order), order)
                for part, m in enumerate((m_high, m_low)):
                    m[s, kind, where, lanes] = split[n, part, from_row, (i + k) % 2, k // 2, :, side]
    for j in range(7, -1, -1):
        first = j // 2 * 128
        for n, s in enumerate(groups):
            after = 8 * order - first - (j % 2 + 1) * order
            row = jnp.pad(pivots[n, j], ((0, 0), (j % 2 * order, after)))
            if j < 7:
                where = [
                    pl.ds(pl.multiple_of(jnp.minimum(o[k] + j, 7) * order, order), order)
                    for k in range(2)
                ]
                right = jnp.concatenate(
                    [w[s, where[k], first:] for w in (w_high, w_low) for k in range(2)], axis=0
                )
                both = lax.dot_general(lefts[n, j], right, NN, preferred_element_type=F32)
                row = row - (both[:order] + both[order:])
            high, low = halves(row)
            w_high[s, j * order : (j + 1) * order, first:] = high
            w_low[s, j * order : (j + 1) * order, first:] = low


def own_factor_kernel(offsets, own, m_high, m_low, w_high, w_low, g_high, g_low, split):
    mats = (m_high, m_low, w_high, w_low, g_high, g_low)
    for ref in mats:
        ref[...] = jnp.zeros_like(ref)
    factors(offsets, [own], split, [lax.axis_index("pos")], *mats)


def factor_kernel(layout, count, ins, mats, outs, scratch):
    offsets, given = ins[0], ins[1:]
    staged, groups = [], []
    for n, (mask, pieces) in enumerate(layout):
        stage = scratch[0].at[n]
        for t in range(count):
            stage_rows(stage, t, [(given[i * count + t], first, rows) for i, first, rows in pieces])
        staged.append(stage)
        groups.append(lax.axis_index("pos") ^ mask)
    factors(offsets, staged, scratch[1], groups, *mats)


def upper(x, high, low):
    half = high.shape[0] // 2
    return jnp.concatenate(
        [
            product(x[:, :half], high[:half, :half], low[:half, :half], NN),
            product(x, high[:, half:], low[:, half:], NN),
        ],
        axis=1,
    )


def upper_t(x, high, low):
    half = high.shape[0] // 2
    return jnp.concatenate(
        [
            product(x, high[:half], low[:half], NT),
            product(x[:, half:], high[half:, half:], low[half:, half:], NT),
        ],
        axis=1,
    )


def lower(x, high, low):
    half = high.shape[0] // 2
    return jnp.concatenate(
        [
            product(x, high[:, :half], low[:, :half], NN),
            product(x[:, half:], high[half:, half:], low[half:, half:], NN),
        ],
        axis=1,
    )


def lower_t(x, high, low):
    half = high.shape[0] // 2
    return jnp.concatenate(
        [
            product(x[:, :half], high[:half, :half], low[:half, :half], NT),
            product(x, high[half:], low[half:], NT),
        ],
        axis=1,
    )


def forward_step(s, source, before, m, w):
    if before is not None:
        source = source - lower(before, m[0].at[s - 1, 0], m[1].at[s - 1, 0])
    value = upper(source, w[0].at[s], w[1].at[s])
    return value, source - upper(value, m[0].at[s, 1], m[1].at[s, 1])


def first_kernel(mats, r, t, top):
    m, w = mats[:2], mats[2:4]
    value = None
    for s in range(8):
        value, t[s] = forward_step(s, r[s], value, m, w)
    z = upper_t(t[7], w[0][7], w[1][7])
    top[0] = z
    top[1] = lower(z, m[0][7, 0], m[1][7, 0])


def spread(out, kind, values, below, above):
    values = [below, *values, above]
    for s in range(8):
        for side in range(3):
            out[s, kind, side] = values[s + side]


def second_kernel(mats, t, top, z, above, ends):
    m, w = mats[:2], mats[2:4]
    value = top[0]
    values = {7: value}
    for s in range(6, -1, -1):
        above[s] = lower_t(value, m[0][s, 0], m[1][s, 0])
        value = upper_t(t[s] - above[s], w[0][s], w[1][s])
        values[s] = value
    above[7] = jnp.zeros_like(value)
    for s in range(8):
        z[s] = values[s]
    ends[:2] = top[...]
    ends[2] = value


def third_kernel(mats, r, t, z, above, source, t_left):
    m, g = mats[:2], mats[4:]
    for s in range(8):
        x = z[s]
        ahead = upper_t(x, m[0][s, 1], m[1][s, 1]) + above[s]
        own = [
            product(x[:, i * 128 : (i + 1) * 128], g[0][s, i], g[1][s, i], NN) for i in range(4)
        ]
        t_left[s] = t[s] - ahead
        source[s] = jnp.concatenate(own, axis=1) + ahead - t_left[s] - r[s]


def fourth_kernel(mats, source, t_left, from_below, from_above, t, last):
    m, w = mats[:2], mats[2:4]
    before = None
    for s in range(8):
        start = source[s]
        if s == 0:
            start = start + from_below[1]
        if s == 7:
            start = start + lower_t(from_above[2], m[0][7, 0], m[1][7, 0])
        before, more = forward_step(s, start, before, m, w)
        t[s] = t_left[s] + more
    last[...] = upper_t(t[7], w[0][7], w[1][7])


def fifth_kernel(mats, t, last, z, from_below, from_above, out):
    m, w = mats[:2], mats[2:4]
    value = last[...]
    values = [value]
    for s in range(6, -1, -1):
        ahead = lower_t(value, m[0][s, 0], m[1][s, 0])
        value = upper_t(t[s] - ahead, w[0][s], w[1][s])
        values.insert(0, value)
    zero = jnp.zeros_like(value)
    spread(out, 0, [z[s] for s in range(8)], from_below[0], from_above[2])
    spread(out, 1, values, zero, zero)


def halo_kernel(rows, arrived, out):
    out[...] = rows[...]
    out[0, 1, 0] = arrived[...]


def place_rows(place, t, rhs, rows, lanes=slice(None)):
    count = rows.shape[0]
    place[pl.ds(pl.multiple_of((rhs ^ t) * count, count), count), lanes] = rows


def inner(a, b):
    return lax.dot_general(a, b, NT, precision=HIGHEST, preferred_element_type=F32)


def products_kernel(n, *refs):
    r_pieces, pieces, bands = refs[:n], refs[n : 2 * n], refs[2 * n : 2 * n + 4]
    r, d, q, e, w, sums, wide = refs[2 * n + 4 :]
    rhs, cells, total = lax.axis_index("rhs"), pieces[0].shape[4], r.shape[0]
    for t in range(n):
        place_rows(r, t, rhs, r_pieces[t][...])
        for kind in range(2):
            for side in range(3):
                rows = jnp.concatenate([pieces[t][j, kind, side] for j in range(SPAN)], axis=0)
                lanes = slice(side * cells, (side + 1) * cells)
                place_rows(wide.at[pl.ds(kind * total, total)], t, rhs, rows, lanes)
    below = along(wide[:, :cells], bands, 0, cells)
    image = below + along(wide[:, cells:], bands, cells, 3 * cells)
    first = jnp.where(lax.axis_index("pos") == 0, 1.0, 0.0)
    below_e = below[total:] * first
    own = slice(cells, 2 * cells)
    d[...], e[...] = wide[:total, own], wide[total:, own]
    q[...], w[...] = image[:total], image[total:]
    odd = rhs % 2 == 1
    left = jnp.where(odd, e[...], d[...])
    rights = jnp.where(odd, q[...], r[...]), jnp.where(odd, w[...] + below_e, q[...])
    sums[...] = jnp.concatenate([inner(left, right) for right in rights], axis=1)


def complete_kernel(value, arrived, *refs):
    cells = value.shape[1]
    refs[4][...] = value[...] + along(arrived[...], refs[:4], 2 * cells, 3 * cells)


def small(a, b):
    return lax.dot_general(a, b, NN, precision=HIGHEST, preferred_element_type=F32)


def inverse(a):
    at = [lax.broadcasted_iota(jnp.int32, a.shape, d) for d in range(2)]
    same = at[0] == at[1]
    eye = jnp.where(same, 1.0, 0.0)
    kept = jnp.where(same, a, 0.0)
    by_row = lax.rsqrt(jnp.sum(kept, axis=1, keepdims=True))
    by_column = lax.rsqrt(jnp.sum(kept, axis=0, keepdims=True))
    a = a * by_row * by_column
    scale = 1.0 / jnp.max(jnp.sum(jnp.abs(a), axis=0, keepdims=True), axis=1, keepdims=True)
    rest = eye - a * scale
    total = eye + rest

    def step(total, rest):
        rest = product(rest, *halves(rest), NN)
        return total + product(total, *halves(rest), NN), rest

    for _ in range(7):
        total, rest = step(total, rest)

    def going(carry):
        turn, _, rest = carry
        return (turn < 40) & (jnp.max(jnp.abs(rest)) > 1e-7)

    def more(carry):
        turn, total, rest = carry
        return (turn + 1, *step(total, rest))

    _, total, _ = lax.while_loop(going, more, (jnp.int32(0), total, rest))
    total = total * scale
    total = total + small(total, eye - small(a, total))
    return total * by_row * by_column


def symmetric(a):
    return 0.5 * (a + a.T)


def last_kernel(own_sums, other_sums, r, d, q, e, w, solution, residual):
    count, total = solution.shape[0], r.shape[0]
    rhs = lax.axis_index("rhs")
    odd = rhs % 2 == 1
    sums = jnp.where(odd, other_sums[...], own_sums[...]), jnp.where(odd, own_sums[...], other_sums[...])
    s1, s2, s3, s4 = [
        symmetric(sums[k // 2][:, k % 2 * total : (k % 2 + 1) * total]) for k in range(4)
    ]
    gram = jnp.concatenate(
        [jnp.concatenate([s2, s3], axis=1), jnp.concatenate([s3, s4], axis=1)], axis=0
    )
    weights = small(jnp.concatenate([s1, s2 - s1], axis=1), inverse(gram))
    pick = lax.broadcasted_iota(jnp.int32, (count, total), 0) + rhs * count
    pick = jnp.where(pick == lax.broadcasted_iota(jnp.int32, pick.shape, 1), 1.0, 0.0)
    weights = small(pick, weights)
    own = r[pl.ds(pl.multiple_of(rhs * count, count), count), :]
    solution[...] = small(weights, jnp.concatenate([d[...], e[...]], axis=0))
    residual[...] = own - small(weights, jnp.concatenate([q[...], w[...]], axis=0))


def swapped(value, axis, bit):
    return lax.ppermute(value, axis, [(i, i ^ bit) for i in range(lax.axis_size(axis))])


def summed(value):
    axes = ("blk", "pos")
    size = lax.axis_size(axes)
    bit = 1
    while bit < size:
        near = value + swapped(value, axes, bit)
        if 2 * bit < size:
            near = near + (swapped(value, axes, 2 * bit) + swapped(value, axes, 3 * bit))
        value = near
        bit *= 4
    return value


def both_ways(value):
    blocks = lax.axis_size("blk")
    low = high = None
    for first in range(min(2, blocks - 1)):
        pairs = [(i, i + 1) for i in range(first, blocks - 1, 2)]
        got = lax.ppermute(value, "blk", pairs + [(b, a) for a, b in pairs])
        even = lax.axis_index("blk") % 2 == first
        up, down = jnp.where(even, 0.0, got), jnp.where(even, got, 0.0)
        low, high = (up, down) if low is None else (low + up, high + down)
    return low, high


def shards(right_side, tiles, pivots, columns):
    count, cells = right_side.shape
    shard_rows, slots, order, _ = tiles.shape
    parts = lax.axis_size("rhs")
    blocks = lax.axis_size("blk")
    rows_part = shard_rows // parts
    each = count // SPAN
    total = count * parts
    S = jax.ShapeDtypeStruct
    up = [(i, i + 1) for i in range(blocks - 1)]
    down_rows = [(SPAN * (i + 1), SPAN * (i + 1) - 1) for i in range(blocks - 1)]

    def others(value):
        return [value] + [swapped(value, "rhs", t) for t in range(1, parts)]

    tall = 2 * order + 8
    own, part, offsets = call(
        functools.partial(pack_kernel, rows_part),
        "pack_tiles",
        [
            S((shard_rows, tall, 2 * order), F32),
            S((rows_part, tall, 2 * order), F32),
            S((1, 3), jnp.int32),
        ],
        [pl.BlockSpec(memory_space=pl.ANY)] * 3,
        [VMEM, VMEM, SMEM],
        [
            pltpu.SMEM(columns.shape, jnp.int32),
            pltpu.VMEM(tiles.shape, F32),
            pltpu.VMEM(pivots.shape, F32),
            pltpu.SemaphoreType.DMA((2 + shard_rows,)),
        ],
        cost=2,
        limit=60,
    )(columns, tiles, pivots)

    vectors, vector = S((SPAN, each, cells), F32), S((each, cells), F32)
    r = lax.all_to_all(right_side.reshape(SPAN, each, cells), "pos", 0, 0, tiled=True)
    x, y, z = (swapped(part, "pos", bit) for bit in (1, 2, 4))
    mat_shapes = [
        pltpu.VMEM((SPAN, 2, cells, cells), BF16),
        pltpu.VMEM((SPAN, 2, cells, cells), BF16),
        pltpu.VMEM((SPAN, cells, cells), BF16),
        pltpu.VMEM((SPAN, cells, cells), BF16),
        pltpu.VMEM((SPAN, 4, 2 * order, 2 * order), BF16),
        pltpu.VMEM((SPAN, 4, 2 * order, 2 * order), BF16),
    ]
    splits = lambda groups: pltpu.VMEM((groups, 2, 8, 2, 2, order, 2 * order), BF16)
    bands = []
    for half in range(2):
        bands += call(
            functools.partial(band_kernel, half * shard_rows // 2),
            "row_band",
            [S((3 * cells, cells // 2), BF16)] * 2,
            [SMEM, VMEM],
            [VMEM] * 2,
            [pltpu.VMEM((3 * cells, cells // 2), F32)],
            cost=20,
        )(columns, tiles)

    own, r = lax.optimization_barrier((own, r))
    mats = call(
        own_factor_kernel,
        "factors_own",
        mat_shapes,
        [SMEM, VMEM],
        [VMEM] * 6,
        [splits(1)],
        cost=4,
    )(offsets, own)
    def with_mats(kernel, name, specs, out_shapes, given, scratch=(), cost=1):
        nonlocal mats
        first, outs = len(given), len(out_shapes)

        def body(*refs):
            ins, rest = refs[:first], refs[first + 6 :]
            kernel(ins, rest[outs : outs + 6], rest[:outs], rest[outs + 6 :])

        *results, m0, m1, w0, w1, g0, g1 = call(
            body,
            name,
            [*out_shapes, *mat_shapes],
            [*specs, *[VMEM] * 6],
            [VMEM] * (outs + 6),
            scratch,
            {first + i: outs + i for i in range(6)},
            cost,
        )(*given, *mats)
        mats = [m0, m1, w0, w1, g0, g1]
        return results

    def add_factors(name, layout, operands, cost):
        given = [offsets] + [piece for operand in operands for piece in others(operand)]
        with_mats(
            functools.partial(factor_kernel, layout, parts),
            name,
            [SMEM] + [VMEM] * (len(given) - 1),
            [],
            given,
            [pltpu.VMEM((len(layout), shard_rows, tall, 2 * order), F32), splits(len(layout))],
            cost,
        )

    def sweep(kernel, name, out_shapes, *given, cost=1):
        def body(ins, held, outs, scratch):
            kernel(held, *ins, *outs)

        return with_mats(body, name, [VMEM] * len(given), out_shapes, given, cost=cost)

    join = lambda *pieces: jnp.concatenate(pieces, axis=1)
    xs = swapped(join(y[:, :order], z[:, :order]), "pos", 1)
    ys = swapped(join(x[:, order:], z[:, :order]), "pos", 2)
    zs = swapped(join(x[:, order:], y[:, order:]), "pos", 4)
    rest = tall - order
    far_top = swapped(ys[:, rest:], "pos", 1)
    far_low = swapped(ys[:, :rest], "pos", 4)
    add_factors(
        "factors_near", [(bit, [(i, 0, tall)]) for i, bit in enumerate((1, 2, 4))], [x, y, z], 6
    )
    add_factors(
        "factors_mid",
        [
            (3, [(0, 0, order), (1, 0, rest)]),
            (5, [(0, order, order), (2, 0, rest)]),
            (6, [(1, rest, order), (2, rest, rest)]),
        ],
        [xs, ys, zs],
        6,
    )
    add_factors("factors_far", [(7, [(0, 0, order), (1, 0, rest)])], [far_top, far_low], 3)

    r_pieces = others(right_side)
    ends_shape, spread_shape = S((3, each, cells), F32), S((SPAN, 2, 3, each, cells), F32)
    t, top = sweep(first_kernel, "forward_r", [vectors, S((2, each, cells), F32)], r, cost=4)
    z, above, ends = sweep(
        second_kernel, "backward_r", [vectors, vectors, ends_shape], t, top, cost=4
    )
    from_below, from_above = both_ways(ends)
    source, t_left = sweep(third_kernel, "residue_of_z", [vectors] * 2, r, t, z, above, cost=2)
    t, last = sweep(
        fourth_kernel, "forward_v", [vectors, vector], source, t_left, from_below, from_above, cost=4
    )
    last_below = lax.ppermute(last, "blk", up)
    (rows,) = sweep(
        fifth_kernel, "backward_v", [spread_shape], t, last, z, from_below, from_above, cost=4
    )
    rows = call(halo_kernel, "halo", spread_shape, [VMEM] * 2)(rows, last_below)
    rows = lax.all_to_all(rows, "pos", 0, 0, tiled=True)

    full, sums_shape = S((total, cells), F32), S((total, 2 * total), F32)
    r_full, d, q, e, w_part, sums = call(
        functools.partial(products_kernel, parts),
        "products",
        [full] * 5 + [sums_shape],
        [VMEM] * (2 * parts + 4),
        [VMEM] * 6,
        [pltpu.VMEM((2 * total, 3 * cells), F32)],
        cost=2,
    )(*r_pieces, *others(rows), *bands)
    sums = summed(sums)
    e_above = lax.ppermute(e, ("blk", "pos"), down_rows)
    w = call(complete_kernel, "complete", full, [VMEM] * 6)(w_part, e_above, *bands)
    return call(last_kernel, "update", [S((count, cells), F32)] * 2, [VMEM] * 7, [VMEM] * 2, cost=8)(
        sums, swapped(sums, "rhs", 1), r_full, d, q, e, w
    )


def solution(mesh):
    devices = mesh.devices
    split = Mesh(
        devices.reshape(devices.shape[0] // SPAN, SPAN, devices.shape[1]), ("blk", "pos", "rhs")
    )
    rows = ("blk", "pos")
    return jax.shard_map(
        shards,
        mesh=split,
        in_specs=(
            P("rhs", rows),
            P(rows, None, None, None),
            P(rows, None, None),
            P(rows, None),
        ),
        out_specs=(P("rhs", rows), P("rhs", rows)),
        check_vma=False,
    )
```

```python
import functools
import jax
import jax.numpy as jnp
from jax import lax
from jax.experimental import pallas as pl
from jax.experimental.pallas import tpu as pltpu
from jax.sharding import Mesh, PartitionSpec as P

SPAN = 8
F32 = jnp.float32
BF16 = jnp.bfloat16
HIGHEST = lax.Precision.HIGHEST
NN = (((1,), (0,)), ((), ()))
NT = (((1,), (1,)), ((), ()))
VMEM = pl.BlockSpec(memory_space=pltpu.VMEM)
SMEM = pl.BlockSpec(memory_space=pltpu.SMEM)


def call(kernel, name, out_shape, in_specs, out_specs=VMEM, scratch=(), aliases=None, cost=1, limit=16):
    return pl.pallas_call(
        kernel,
        out_shape=out_shape,
        in_specs=in_specs,
        out_specs=out_specs,
        scratch_shapes=list(scratch),
        input_output_aliases=aliases or {},
        cost_estimate=pl.CostEstimate(flops=int(cost * 1e9), bytes_accessed=0, transcendentals=0),
        compiler_params=pltpu.CompilerParams(vmem_limit_bytes=limit * 2**20),
        name=name,
    )


def two_parts(x):
    high = x.astype(BF16).astype(F32)
    return jnp.concatenate([high, x - high], axis=0).astype(BF16)


def halves(x):
    high = x.astype(BF16)
    return high, (x - high.astype(F32)).astype(BF16)


def product(x, high, low, dims):
    parts = two_parts(x)
    both = lax.dot_general(parts, high, dims, preferred_element_type=F32)
    both = both + lax.dot_general(parts, low, dims, preferred_element_type=F32)
    rows = x.shape[0]
    return both[:rows] + both[rows:]


def offsets_of(columns, start):
    found = []
    for offset in range(1, 8):
        hit = jnp.int32(0)
        for slot in range(7):
            away = columns[0, slot] - start
            hit = hit | jnp.where((away == offset) | (away == -offset), 1, 0)
        found.append(hit * 16 + offset)
    first = functools.reduce(jnp.maximum, found)
    second = functools.reduce(jnp.maximum, [jnp.where(f == first, 0, f) for f in found])
    first, second = (first & 15, second & 15)
    return (jnp.minimum(first, second), jnp.maximum(first, second), jnp.int32(8))


def pack_kernel(rows_part, columns_far, tiles_far, pivots_far, own, part, offsets, *scratch):
    columns, tiles, pivots, sems = scratch
    shard_rows, slots, order, _ = tiles.shape
    copies = [
        pltpu.make_async_copy(far, near, sems.at[i])
        for i, (far, near) in enumerate(((columns_far, columns), (pivots_far, pivots)))
    ]
    for row in range(shard_rows):
        copies.append(pltpu.make_async_copy(tiles_far.at[row], tiles.at[row], sems.at[2 + row]))
    for copy in copies:
        copy.start()
    copies[0].wait()
    start = (lax.axis_index("blk") * SPAN + lax.axis_index("pos")) * shard_rows
    offs = offsets_of(columns, start)
    for k in range(3):
        offsets[0, k] = offs[k]
    at = [lax.broadcasted_iota(jnp.int32, (order, order), d) for d in range(2)]
    copies[1].wait()
    for row in range(shard_rows):
        copies[2 + row].wait()
        sums = [jnp.zeros((order, order), F32) for _ in range(4)]
        for slot in range(slots):
            away = columns[row, slot] - (start + row)
            tile = tiles[row, slot]
            for k, want in enumerate((*offs, 0)):
                sums[k] = sums[k] + tile * jnp.where(away == want, 1.0, 0.0)
        both = jnp.where(at[0] <= at[1], pivots[row], sums[3])
        line = jnp.sum(jnp.where(at[0] == at[1], sums[3], 0.0), axis=0, keepdims=True)
        own[row, :order] = jnp.concatenate([sums[0], sums[1]], axis=1)
        own[row, order : 2 * order] = jnp.concatenate([sums[2], both], axis=1)
        own[row, 2 * order :] = jnp.broadcast_to(jnp.concatenate([line, line], axis=1), (8, 2 * order))
    for a in range(rows_part):
        part[a] = own[lax.axis_index("rhs") * rows_part + a]


def band_kernel(first_row, columns, tiles, band_high, band_low, band):
    shard_rows, slots, order, _ = tiles.shape
    start = (lax.axis_index("blk") * SPAN + lax.axis_index("pos")) * shard_rows
    band[...] = jnp.zeros_like(band)
    for row in range(shard_rows // 2):
        for slot in range(slots):
            away = columns[first_row + row, slot] - start + shard_rows
            where = pl.ds(pl.multiple_of(away * order, order), order)
            lanes = pl.ds(row * order, order)
            band[where, lanes] = band[where, lanes] + tiles[first_row + row, slot].T
    high, low = halves(band[...])
    band_high[...] = high
    band_low[...] = low


def along(x, bands, first, last):
    return jnp.concatenate(
        [product(x, high[first:last], low[first:last], NN) for high, low in zip(bands[::2], bands[1::2])],
        axis=1,
    )


def stage_rows(stage, t, pieces):
    rows_part = pieces[0][0].shape[0]
    base = (lax.axis_index("rhs") ^ t) * rows_part
    for r in range(rows_part):
        top = 0
        for ref, first, rows in pieces:
            stage[base + r, top : top + rows] = ref[r, first : first + rows]
            top += rows


def factors(offsets, stages, split, groups, m_high, m_low, w_high, w_low, g_high, g_low):
    order = 64
    o = [offsets[0, k] for k in range(3)]
    at = [lax.broadcasted_iota(jnp.int32, (order, order), d) for d in range(2)]
    lane = lax.broadcasted_iota(jnp.int32, (order, 2 * order), 1)
    pivots, lefts = {}, {}
    for n, (stage, s) in enumerate(zip(stages, groups)):
        for i in range(8):
            for p in range(2):
                pair = stage[i, p * order : (p + 1) * order]
                turned = jnp.concatenate([pair[:, order:], pair[:, :order]], axis=1)
                for version, tiles in enumerate((pair, turned)):
                    split[n, 0, i, version, p], split[n, 1, i, version, p] = halves(tiles)
            both = stage[i, order : 2 * order, order:]
            turned = both.T
            pivots[n, i] = jnp.where(at[0] <= at[1], both, turned)
            line = stage[i, 2 * order : 2 * order + 1, :order]
            tile = jnp.where(at[0] > at[1], both, jnp.where(at[0] < at[1], turned, line))
            high, low = halves(tile)
            where = slice(i % 2 * order, (i % 2 + 1) * order)
            g_high[s, i // 2, where, where] = high
            g_low[s, i // 2, where, where] = low
        for j in range(7):
            inside = [jnp.where(o[k] + j <= 7, 1.0, 0.0) for k in range(2)]
            pair = stage[j, :order] * jnp.where(lane < order, inside[0], inside[1])
            left = two_parts(product(pivots[n, j], *halves(pair), NN))
            lefts[n, j] = jnp.concatenate([left, left], axis=1)
        for i in range(8):
            lanes = slice(i * order, (i + 1) * order)
            side = slice(i % 2 * order, (i % 2 + 1) * order)
            for k in range(3):
                from_row = (i - o[k]) & 7 if k < 2 else i
                kind = jnp.where(o[k] > i, 0, 1) if k < 2 else 0
                where = pl.ds(pl.multiple_of(from_row * order, order), order)
                for part, m in enumerate((m_high, m_low)):
                    m[s, kind, where, lanes] = split[n, part, from_row, (i + k) % 2, k // 2, :, side]
    for j in range(7, -1, -1):
        first = j // 2 * 128
        for n, s in enumerate(groups):
            after = 8 * order - first - (j % 2 + 1) * order
            row = jnp.pad(pivots[n, j], ((0, 0), (j % 2 * order, after)))
            if j < 7:
                where = [
                    pl.ds(pl.multiple_of(jnp.minimum(o[k] + j, 7) * order, order), order)
                    for k in range(2)
                ]
                right = jnp.concatenate(
                    [w[s, where[k], first:] for w in (w_high, w_low) for k in range(2)], axis=0
                )
                both = lax.dot_general(lefts[n, j], right, NN, preferred_element_type=F32)
                row = row - (both[:order] + both[order:])
            high, low = halves(row)
            w_high[s, j * order : (j + 1) * order, first:] = high
            w_low[s, j * order : (j + 1) * order, first:] = low


def own_factor_kernel(offsets, own, m_high, m_low, w_high, w_low, g_high, g_low, split):
    mats = (m_high, m_low, w_high, w_low, g_high, g_low)
    half = m_high.shape[2] // 2
    for ref in (m_high, m_low):
        for kind in range(2):
            ref[:, kind, :half, : half * (1 + kind)] = jnp.zeros((SPAN, half, half * (1 + kind)), BF16)
            ref[:, kind, half:, half * kind :] = jnp.zeros((SPAN, half, half * (2 - kind)), BF16)
    for ref in mats[2:]:
        ref[...] = jnp.zeros_like(ref)
    factors(offsets, [own], split, [lax.axis_index("pos")], *mats)


def factor_kernel(layout, count, ins, mats, outs, scratch):
    offsets, given = ins[0], ins[1:]
    staged, groups = [], []
    for n, (mask, pieces) in enumerate(layout):
        stage = scratch[0].at[n]
        for t in range(count):
            stage_rows(stage, t, [(given[i * count + t], first, rows) for i, first, rows in pieces])
        staged.append(stage)
        groups.append(lax.axis_index("pos") ^ mask)
    factors(offsets, staged, scratch[1], groups, *mats)


def upper(x, high, low):
    half = high.shape[0] // 2
    return jnp.concatenate(
        [
            product(x[:, :half], high[:half, :half], low[:half, :half], NN),
            product(x, high[:, half:], low[:, half:], NN),
        ],
        axis=1,
    )


def upper_t(x, high, low):
    half = high.shape[0] // 2
    return jnp.concatenate(
        [
            product(x, high[:half], low[:half], NT),
            product(x[:, half:], high[half:, half:], low[half:, half:], NT),
        ],
        axis=1,
    )


def lower(x, high, low):
    half = high.shape[0] // 2
    return jnp.concatenate(
        [
            product(x, high[:, :half], low[:, :half], NN),
            product(x[:, half:], high[half:, half:], low[half:, half:], NN),
        ],
        axis=1,
    )


def lower_t(x, high, low):
    half = high.shape[0] // 2
    return jnp.concatenate(
        [
            product(x[:, :half], high[:half, :half], low[:half, :half], NT),
            product(x, high[half:], low[half:], NT),
        ],
        axis=1,
    )


def forward_step(s, source, before, m, w):
    if before is not None:
        source = source - lower(before, m[0].at[s - 1, 0], m[1].at[s - 1, 0])
    value = upper(source, w[0].at[s], w[1].at[s])
    return value, source - upper(value, m[0].at[s, 1], m[1].at[s, 1])


def first_kernel(mats, r, t, top):
    m, w = mats[:2], mats[2:4]
    value = None
    for s in range(8):
        value, t[s] = forward_step(s, r[s], value, m, w)
    z = upper_t(t[7], w[0][7], w[1][7])
    top[0] = z
    top[1] = lower(z, m[0][7, 0], m[1][7, 0])


def spread(out, kind, values, below, above):
    values = [below, *values, above]
    for s in range(8):
        for side in range(3):
            out[s, kind, side] = values[s + side]


def second_kernel(mats, t, top, z, above, ends):
    m, w = mats[:2], mats[2:4]
    value = top[0]
    values = {7: value}
    for s in range(6, -1, -1):
        above[s] = lower_t(value, m[0][s, 0], m[1][s, 0])
        value = upper_t(t[s] - above[s], w[0][s], w[1][s])
        values[s] = value
    above[7] = jnp.zeros_like(value)
    for s in range(8):
        z[s] = values[s]
    ends[:2] = top[...]
    ends[2] = value


def third_kernel(mats, r, t, z, above, source, t_left):
    m, g = mats[:2], mats[4:]
    for s in range(8):
        x = z[s]
        ahead = upper_t(x, m[0][s, 1], m[1][s, 1]) + above[s]
        own = [
            product(x[:, i * 128 : (i + 1) * 128], g[0][s, i], g[1][s, i], NN) for i in range(4)
        ]
        t_left[s] = t[s] - ahead
        source[s] = jnp.concatenate(own, axis=1) + ahead - t_left[s] - r[s]


def fourth_kernel(mats, source, t_left, from_below, from_above, t, last):
    m, w = mats[:2], mats[2:4]
    before = None
    for s in range(8):
        start = source[s]
        if s == 0:
            start = start + from_below[1]
        if s == 7:
            start = start + lower_t(from_above[2], m[0][7, 0], m[1][7, 0])
        before, more = forward_step(s, start, before, m, w)
        t[s] = t_left[s] + more
    last[...] = upper_t(t[7], w[0][7], w[1][7])


def fifth_kernel(mats, t, last, z, from_below, from_above, out):
    m, w = mats[:2], mats[2:4]
    value = last[...]
    values = [value]
    for s in range(6, -1, -1):
        ahead = lower_t(value, m[0][s, 0], m[1][s, 0])
        value = upper_t(t[s] - ahead, w[0][s], w[1][s])
        values.insert(0, value)
    zero = jnp.zeros_like(value)
    spread(out, 0, [z[s] for s in range(8)], from_below[0], from_above[2])
    spread(out, 1, values, zero, zero)


def halo_kernel(rows, *refs):
    out, odd = refs[-1], lax.axis_index("blk") % 2
    out[...] = rows[...]
    for n, got in enumerate(refs[:-1]):
        out[0, 1, 0] += got[...] * jnp.where(odd == n, 0.0, 1.0)


def place_rows(place, t, rhs, rows, lanes=slice(None)):
    count = rows.shape[0]
    place[pl.ds(pl.multiple_of((rhs ^ t) * count, count), count), lanes] = rows


def inner(a, b):
    return lax.dot_general(a, b, NT, precision=HIGHEST, preferred_element_type=F32)


def products_kernel(n, *refs):
    r_pieces, pieces, bands = refs[:n], refs[n : 2 * n], refs[2 * n : 2 * n + 4]
    r, d, q, e, w, sums, wide = refs[2 * n + 4 :]
    rhs, cells, total = lax.axis_index("rhs"), pieces[0].shape[4], r.shape[0]
    for t in range(n):
        place_rows(r, t, rhs, r_pieces[t][...])
        for kind in range(2):
            for side in range(3):
                rows = jnp.concatenate([pieces[t][j, kind, side] for j in range(SPAN)], axis=0)
                lanes = slice(side * cells, (side + 1) * cells)
                place_rows(wide.at[pl.ds(kind * total, total)], t, rhs, rows, lanes)
    below = along(wide[:, :cells], bands, 0, cells)
    image = below + along(wide[:, cells:], bands, cells, 3 * cells)
    first = jnp.where(lax.axis_index("pos") == 0, 1.0, 0.0)
    below_e = below[total:] * first
    own = slice(cells, 2 * cells)
    d[...], e[...] = wide[:total, own], wide[total:, own]
    q[...], w[...] = image[:total], image[total:]
    odd = rhs % 2 == 1
    left = jnp.where(odd, e[...], d[...])
    rights = jnp.where(odd, q[...], r[...]), jnp.where(odd, w[...] + below_e, q[...])
    sums[...] = jnp.concatenate([inner(left, right) for right in rights], axis=1)


def complete_kernel(value, arrived, *refs):
    cells = value.shape[1]
    refs[4][...] = value[...] + along(arrived[...], refs[:4], 2 * cells, 3 * cells)


def small(a, b):
    return lax.dot_general(a, b, NN, precision=HIGHEST, preferred_element_type=F32)


def inverse(a):
    at = [lax.broadcasted_iota(jnp.int32, a.shape, d) for d in range(2)]
    same = at[0] == at[1]
    eye = jnp.where(same, 1.0, 0.0)
    kept = jnp.where(same, a, 0.0)
    by_row = lax.rsqrt(jnp.sum(kept, axis=1, keepdims=True))
    by_column = lax.rsqrt(jnp.sum(kept, axis=0, keepdims=True))
    a = a * by_row * by_column
    scale = 1.0 / jnp.max(jnp.sum(jnp.abs(a), axis=0, keepdims=True), axis=1, keepdims=True)
    rest = eye - a * scale
    total = eye + rest

    def step(total, rest):
        rest = product(rest, *halves(rest), NN)
        return total + product(total, *halves(rest), NN), rest

    for _ in range(7):
        total, rest = step(total, rest)

    def going(carry):
        turn, _, rest = carry
        return (turn < 40) & (jnp.max(jnp.abs(rest)) > 1e-7)

    def more(carry):
        turn, total, rest = carry
        return (turn + 1, *step(total, rest))

    _, total, _ = lax.while_loop(going, more, (jnp.int32(0), total, rest))
    total = total * scale
    total = total + small(total, eye - small(a, total))
    return total * by_row * by_column


def symmetric(a):
    return 0.5 * (a + a.T)


def last_kernel(own_sums, other_sums, r, d, q, e, w, solution, residual, all_weights):
    count, total = solution.shape[0], r.shape[0]
    rhs = lax.axis_index("rhs")
    odd = rhs % 2 == 1
    sums = jnp.where(odd, other_sums[...], own_sums[...]), jnp.where(odd, own_sums[...], other_sums[...])
    s1, s2, s3, s4 = [
        symmetric(sums[k // 2][:, k % 2 * total : (k % 2 + 1) * total]) for k in range(4)
    ]
    gram = jnp.concatenate(
        [jnp.concatenate([s2, s3], axis=1), jnp.concatenate([s3, s4], axis=1)], axis=0
    )
    weights = small(jnp.concatenate([s1, s2 - s1], axis=1), inverse(gram))
    all_weights[...] = weights
    weights = all_weights[pl.ds(pl.multiple_of(rhs * count, count), count), :]
    own = r[pl.ds(pl.multiple_of(rhs * count, count), count), :]
    solution[...] = small(weights, jnp.concatenate([d[...], e[...]], axis=0))
    residual[...] = own - small(weights, jnp.concatenate([q[...], w[...]], axis=0))


def swapped(value, axis, bit):
    return lax.ppermute(value, axis, [(i, i ^ bit) for i in range(lax.axis_size(axis))])


def summed(value):
    axes = ("blk", "pos")
    size = lax.axis_size(axes)
    bit = 1
    while bit < size:
        near = value + swapped(value, axes, bit)
        if 2 * bit < size:
            near = near + (swapped(value, axes, 2 * bit) + swapped(value, axes, 3 * bit))
        value = near
        bit *= 4
    return value


def exchanged(value):
    blocks, got = lax.axis_size("blk"), []
    for first in range(min(2, blocks - 1)):
        pairs = [(i, i + 1) for i in range(first, blocks - 1, 2)]
        got.append(lax.ppermute(value, "blk", pairs + [(b, a) for a, b in pairs]))
    return got


def both_ways(value):
    low = high = None
    for first, got in enumerate(exchanged(value)):
        even = lax.axis_index("blk") % 2 == first
        up, down = jnp.where(even, 0.0, got), jnp.where(even, got, 0.0)
        low, high = (up, down) if low is None else (low + up, high + down)
    return low, high


def shards(right_side, tiles, pivots, columns):
    count, cells = right_side.shape
    shard_rows, slots, order, _ = tiles.shape
    parts = lax.axis_size("rhs")
    blocks = lax.axis_size("blk")
    rows_part = shard_rows // parts
    each = count // SPAN
    total = count * parts
    S = jax.ShapeDtypeStruct
    down_rows = [(SPAN * (i + 1), SPAN * (i + 1) - 1) for i in range(blocks - 1)]

    def others(value):
        return [value] + [swapped(value, "rhs", t) for t in range(1, parts)]

    tall = 2 * order + 8
    own, part, offsets = call(
        functools.partial(pack_kernel, rows_part),
        "pack_tiles",
        [
            pltpu.VMEM((shard_rows, tall, 2 * order), F32),
            S((rows_part, tall, 2 * order), F32),
            S((1, 3), jnp.int32),
        ],
        [pl.BlockSpec(memory_space=pl.ANY)] * 3,
        [VMEM, VMEM, SMEM],
        [
            pltpu.SMEM(columns.shape, jnp.int32),
            pltpu.VMEM(tiles.shape, F32),
            pltpu.VMEM(pivots.shape, F32),
            pltpu.SemaphoreType.DMA((2 + shard_rows,)),
        ],
        cost=2,
        limit=60,
    )(columns, tiles, pivots)

    vectors, vector = S((SPAN, each, cells), F32), S((each, cells), F32)
    r = lax.all_to_all(right_side.reshape(SPAN, each, cells), "pos", 0, 0, tiled=True)
    x, y, z = (swapped(part, "pos", bit) for bit in (1, 2, 4))
    mat_shapes = [
        pltpu.VMEM((SPAN, 2, cells, cells), BF16),
        pltpu.VMEM((SPAN, 2, cells, cells), BF16),
        pltpu.VMEM((SPAN, cells, cells), BF16),
        pltpu.VMEM((SPAN, cells, cells), BF16),
        pltpu.VMEM((SPAN, 4, 2 * order, 2 * order), BF16),
        pltpu.VMEM((SPAN, 4, 2 * order, 2 * order), BF16),
    ]
    splits = lambda groups: pltpu.VMEM((groups, 2, 8, 2, 2, order, 2 * order), BF16)
    bands = []
    for half in range(2):
        bands += call(
            functools.partial(band_kernel, half * shard_rows // 2),
            "row_band",
            [S((3 * cells, cells // 2), BF16)] * 2,
            [SMEM, VMEM],
            [VMEM] * 2,
            [pltpu.VMEM((3 * cells, cells // 2), F32)],
            cost=20,
        )(columns, tiles)

    own, r = lax.optimization_barrier((own, r))
    mats = call(
        own_factor_kernel,
        "factors_own",
        mat_shapes,
        [SMEM, VMEM],
        [VMEM] * 6,
        [splits(1)],
        cost=4,
    )(offsets, own)
    def with_mats(kernel, name, specs, out_shapes, given, scratch=(), cost=1):
        nonlocal mats
        first, outs = len(given), len(out_shapes)

        def body(*refs):
            ins, rest = refs[:first], refs[first + 6 :]
            kernel(ins, rest[outs : outs + 6], rest[:outs], rest[outs + 6 :])

        *results, m0, m1, w0, w1, g0, g1 = call(
            body,
            name,
            [*out_shapes, *mat_shapes],
            [*specs, *[VMEM] * 6],
            [VMEM] * (outs + 6),
            scratch,
            {first + i: outs + i for i in range(6)},
            cost,
        )(*given, *mats)
        mats = [m0, m1, w0, w1, g0, g1]
        return results

    def add_factors(name, layout, operands, cost):
        given = [offsets] + [piece for operand in operands for piece in others(operand)]
        with_mats(
            functools.partial(factor_kernel, layout, parts),
            name,
            [SMEM] + [VMEM] * (len(given) - 1),
            [],
            given,
            [pltpu.VMEM((len(layout), shard_rows, tall, 2 * order), F32), splits(len(layout))],
            cost,
        )

    def sweep(kernel, name, out_shapes, *given, cost=1):
        def body(ins, held, outs, scratch):
            kernel(held, *ins, *outs)

        return with_mats(body, name, [VMEM] * len(given), out_shapes, given, cost=cost)

    join = lambda *pieces: jnp.concatenate(pieces, axis=1)
    xs = swapped(join(y[:, :order], z[:, :order]), "pos", 1)
    ys = swapped(join(x[:, order:], z[:, :order]), "pos", 2)
    zs = swapped(join(x[:, order:], y[:, order:]), "pos", 4)
    rest = tall - order
    far_top = swapped(ys[:, rest:], "pos", 1)
    far_low = swapped(ys[:, :rest], "pos", 4)
    add_factors(
        "factors_near", [(bit, [(i, 0, tall)]) for i, bit in enumerate((1, 2, 4))], [x, y, z], 6
    )
    add_factors(
        "factors_mid",
        [
            (3, [(0, 0, order), (1, 0, rest)]),
            (5, [(0, order, order), (2, 0, rest)]),
            (6, [(1, rest, order), (2, rest, rest)]),
        ],
        [xs, ys, zs],
        6,
    )
    add_factors("factors_far", [(7, [(0, 0, order), (1, 0, rest)])], [far_top, far_low], 3)

    r_pieces = others(right_side)
    ends_shape, spread_shape = S((3, each, cells), F32), S((SPAN, 2, 3, each, cells), F32)
    t, top = sweep(first_kernel, "forward_r", [vectors, S((2, each, cells), F32)], r, cost=4)
    z, above, ends = sweep(
        second_kernel, "backward_r", [vectors, vectors, ends_shape], t, top, cost=4
    )
    from_below, from_above = both_ways(ends)
    source, t_left = sweep(third_kernel, "residue_of_z", [vectors] * 2, r, t, z, above, cost=2)
    t, last = sweep(
        fourth_kernel, "forward_v", [vectors, vector], source, t_left, from_below, from_above, cost=4
    )
    halos = exchanged(last)
    (rows,) = sweep(
        fifth_kernel, "backward_v", [spread_shape], t, last, z, from_below, from_above, cost=4
    )
    rows = call(halo_kernel, "halo", spread_shape, [VMEM] * (1 + len(halos)))(rows, *halos)
    rows = lax.all_to_all(rows, "pos", 0, 0, tiled=True)

    full, sums_shape = S((total, cells), F32), S((total, 2 * total), F32)
    r_full, d, q, e, w_part, sums = call(
        functools.partial(products_kernel, parts),
        "products",
        [full] * 5 + [sums_shape],
        [VMEM] * (2 * parts + 4),
        [VMEM] * 6,
        [pltpu.VMEM((2 * total, 3 * cells), F32)],
        cost=2,
    )(*r_pieces, *others(rows), *bands)
    sums = summed(sums)
    e_above = lax.ppermute(e, ("blk", "pos"), down_rows)
    w = call(complete_kernel, "complete", full, [VMEM] * 6)(w_part, e_above, *bands)
    return call(
        last_kernel,
        "update",
        [S((count, cells), F32)] * 2,
        [VMEM] * 7,
        [VMEM] * 2,
        [pltpu.VMEM((total, 2 * total), F32)],
        cost=5,
    )(sums, swapped(sums, "rhs", 1), r_full, d, q, e, w)


def solution(mesh):
    devices = mesh.devices
    split = Mesh(
        devices.reshape(devices.shape[0] // SPAN, SPAN, devices.shape[1]), ("blk", "pos", "rhs")
    )
    rows = ("blk", "pos")
    return jax.shard_map(
        shards,
        mesh=split,
        in_specs=(
            P("rhs", rows),
            P(rows, None, None, None),
            P(rows, None, None),
            P(rows, None),
        ),
        out_specs=(P("rhs", rows), P("rhs", rows)),
        check_vma=False,
    )
```

```python
import functools
import jax
import jax.numpy as jnp
from jax import lax
from jax.experimental import pallas as pl
from jax.experimental.pallas import tpu as pltpu
from jax.sharding import Mesh, PartitionSpec as P

SPAN = 8
F32 = jnp.float32
BF16 = jnp.bfloat16
HIGHEST = lax.Precision.HIGHEST
NN = (((1,), (0,)), ((), ()))
NT = (((1,), (1,)), ((), ()))
VMEM = pl.BlockSpec(memory_space=pltpu.VMEM)
SMEM = pl.BlockSpec(memory_space=pltpu.SMEM)


def call(kernel, name, out_shape, in_specs, out_specs=VMEM, scratch=(), aliases=None, cost=1, limit=16):
    return pl.pallas_call(
        kernel,
        out_shape=out_shape,
        in_specs=in_specs,
        out_specs=out_specs,
        scratch_shapes=list(scratch),
        input_output_aliases=aliases or {},
        cost_estimate=pl.CostEstimate(flops=int(cost * 1e9), bytes_accessed=0, transcendentals=0),
        compiler_params=pltpu.CompilerParams(vmem_limit_bytes=limit * 2**20),
        name=name,
    )


def two_parts(x):
    high = x.astype(BF16).astype(F32)
    return jnp.concatenate([high, x - high], axis=0).astype(BF16)


def halves(x):
    high = x.astype(BF16)
    return high, (x - high.astype(F32)).astype(BF16)


def product(x, high, low, dims):
    parts = two_parts(x)
    both = lax.dot_general(parts, high, dims, preferred_element_type=F32)
    both = both + lax.dot_general(parts, low, dims, preferred_element_type=F32)
    rows = x.shape[0]
    return both[:rows] + both[rows:]


def offsets_of(columns, start):
    found = []
    for offset in range(1, 8):
        hit = jnp.int32(0)
        for slot in range(7):
            away = columns[0, slot] - start
            hit = hit | jnp.where((away == offset) | (away == -offset), 1, 0)
        found.append(hit * 16 + offset)
    first = functools.reduce(jnp.maximum, found)
    second = functools.reduce(jnp.maximum, [jnp.where(f == first, 0, f) for f in found])
    first, second = (first & 15, second & 15)
    return (jnp.minimum(first, second), jnp.maximum(first, second), jnp.int32(8))


def pack_kernel(rows_part, columns_far, tiles_far, pivots_far, own, part, offsets, *scratch):
    columns, tiles, pivots, sems = scratch
    shard_rows, slots, order, _ = tiles.shape
    copies = [
        pltpu.make_async_copy(far, near, sems.at[i])
        for i, (far, near) in enumerate(((columns_far, columns), (pivots_far, pivots)))
    ]
    for row in range(shard_rows):
        copies.append(pltpu.make_async_copy(tiles_far.at[row], tiles.at[row], sems.at[2 + row]))
    for copy in copies:
        copy.start()
    copies[0].wait()
    start = (lax.axis_index("blk") * SPAN + lax.axis_index("pos")) * shard_rows
    offs = offsets_of(columns, start)
    for k in range(3):
        offsets[0, k] = offs[k]
    at = [lax.broadcasted_iota(jnp.int32, (order, order), d) for d in range(2)]
    copies[1].wait()
    for row in range(shard_rows):
        copies[2 + row].wait()
        sums = [jnp.zeros((order, order), F32) for _ in range(4)]
        for slot in range(slots):
            away = columns[row, slot] - (start + row)
            tile = tiles[row, slot]
            for k, want in enumerate((*offs, 0)):
                sums[k] = sums[k] + tile * jnp.where(away == want, 1.0, 0.0)
        both = jnp.where(at[0] <= at[1], pivots[row], sums[3])
        line = jnp.sum(jnp.where(at[0] == at[1], sums[3], 0.0), axis=0, keepdims=True)
        own[row, :order] = jnp.concatenate([sums[0], sums[1]], axis=1)
        own[row, order : 2 * order] = jnp.concatenate([sums[2], both], axis=1)
        own[row, 2 * order :] = jnp.broadcast_to(jnp.concatenate([line, line], axis=1), (8, 2 * order))
    for a in range(rows_part):
        part[a] = own[lax.axis_index("rhs") * rows_part + a]


def band_kernel(first_row, columns, tiles, band_high, band_low, band):
    shard_rows, slots, order, _ = tiles.shape
    start = (lax.axis_index("blk") * SPAN + lax.axis_index("pos")) * shard_rows
    band[...] = jnp.zeros_like(band)
    for row in range(shard_rows // 2):
        for slot in range(slots):
            away = columns[first_row + row, slot] - start + shard_rows
            where = pl.ds(pl.multiple_of(away * order, order), order)
            lanes = pl.ds(row * order, order)
            band[where, lanes] = band[where, lanes] + tiles[first_row + row, slot].T
    high, low = halves(band[...])
    band_high[...] = high
    band_low[...] = low


def along(x, bands, first, last):
    return jnp.concatenate(
        [product(x, high[first:last], low[first:last], NN) for high, low in zip(bands[::2], bands[1::2])],
        axis=1,
    )


def stage_rows(stage, t, pieces):
    rows_part = pieces[0][0].shape[0]
    base = (lax.axis_index("rhs") ^ t) * rows_part
    for r in range(rows_part):
        top = 0
        for ref, first, rows in pieces:
            stage[base + r, top : top + rows] = ref[r, first : first + rows]
            top += rows


def factors(offsets, stages, split, groups, m_high, m_low, w_high, w_low, g_high, g_low):
    order = 64
    o = [offsets[0, k] for k in range(3)]
    at = [lax.broadcasted_iota(jnp.int32, (order, order), d) for d in range(2)]
    lane = lax.broadcasted_iota(jnp.int32, (order, 2 * order), 1)
    pivots, lefts = {}, {}
    for n, (stage, s) in enumerate(zip(stages, groups)):
        for i in range(8):
            for p in range(2):
                pair = stage[i, p * order : (p + 1) * order]
                turned = jnp.concatenate([pair[:, order:], pair[:, :order]], axis=1)
                for version, tiles in enumerate((pair, turned)):
                    split[n, 0, i, version, p], split[n, 1, i, version, p] = halves(tiles)
            both = stage[i, order : 2 * order, order:]
            turned = both.T
            pivots[n, i] = jnp.where(at[0] <= at[1], both, turned)
            line = stage[i, 2 * order : 2 * order + 1, :order]
            tile = jnp.where(at[0] > at[1], both, jnp.where(at[0] < at[1], turned, line))
            high, low = halves(tile)
            where = slice(i % 2 * order, (i % 2 + 1) * order)
            g_high[s, i // 2, where, where] = high
            g_low[s, i // 2, where, where] = low
        for j in range(7):
            inside = [jnp.where(o[k] + j <= 7, 1.0, 0.0) for k in range(2)]
            pair = stage[j, :order] * jnp.where(lane < order, inside[0], inside[1])
            left = two_parts(product(pivots[n, j], *halves(pair), NN))
            lefts[n, j] = jnp.concatenate([left, left], axis=1)
        for i in range(8):
            lanes = slice(i * order, (i + 1) * order)
            side = slice(i % 2 * order, (i % 2 + 1) * order)
            for k in range(3):
                from_row = (i - o[k]) & 7 if k < 2 else i
                kind = jnp.where(o[k] > i, 0, 1) if k < 2 else 0
                where = pl.ds(pl.multiple_of(from_row * order, order), order)
                for part, m in enumerate((m_high, m_low)):
                    m[s, kind, where, lanes] = split[n, part, from_row, (i + k) % 2, k // 2, :, side]
    for j in range(7, -1, -1):
        first = j // 2 * 128
        for n, s in enumerate(groups):
            after = 8 * order - first - (j % 2 + 1) * order
            row = jnp.pad(pivots[n, j], ((0, 0), (j % 2 * order, after)))
            if j < 7:
                where = [
                    pl.ds(pl.multiple_of(jnp.minimum(o[k] + j, 7) * order, order), order)
                    for k in range(2)
                ]
                right = jnp.concatenate(
                    [w[s, where[k], first:] for w in (w_high, w_low) for k in range(2)], axis=0
                )
                both = lax.dot_general(lefts[n, j], right, NN, preferred_element_type=F32)
                row = row - (both[:order] + both[order:])
            high, low = halves(row)
            w_high[s, j * order : (j + 1) * order, first:] = high
            w_low[s, j * order : (j + 1) * order, first:] = low


def own_factor_kernel(offsets, own, m_high, m_low, w_high, w_low, g_high, g_low, split):
    mats = (m_high, m_low, w_high, w_low, g_high, g_low)
    half = m_high.shape[2] // 2
    for ref in (m_high, m_low):
        for kind in range(2):
            ref[:, kind, :half, : half * (1 + kind)] = jnp.zeros((SPAN, half, half * (1 + kind)), BF16)
            ref[:, kind, half:, half * kind :] = jnp.zeros((SPAN, half, half * (2 - kind)), BF16)
    for ref in mats[2:]:
        ref[...] = jnp.zeros_like(ref)
    factors(offsets, [own], split, [lax.axis_index("pos")], *mats)


def factor_kernel(layout, count, ins, mats, outs, scratch):
    offsets, given = ins[0], ins[1:]
    staged, groups = [], []
    for n, (mask, pieces) in enumerate(layout):
        stage = scratch[0].at[n]
        for t in range(count):
            stage_rows(stage, t, [(given[i * count + t], first, rows) for i, first, rows in pieces])
        staged.append(stage)
        groups.append(lax.axis_index("pos") ^ mask)
    factors(offsets, staged, scratch[1], groups, *mats)


def upper(x, high, low):
    half = high.shape[0] // 2
    return jnp.concatenate(
        [
            product(x[:, :half], high[:half, :half], low[:half, :half], NN),
            product(x, high[:, half:], low[:, half:], NN),
        ],
        axis=1,
    )


def upper_t(x, high, low):
    half = high.shape[0] // 2
    return jnp.concatenate(
        [
            product(x, high[:half], low[:half], NT),
            product(x[:, half:], high[half:, half:], low[half:, half:], NT),
        ],
        axis=1,
    )


def lower(x, high, low):
    half = high.shape[0] // 2
    return jnp.concatenate(
        [
            product(x, high[:, :half], low[:, :half], NN),
            product(x[:, half:], high[half:, half:], low[half:, half:], NN),
        ],
        axis=1,
    )


def lower_t(x, high, low):
    half = high.shape[0] // 2
    return jnp.concatenate(
        [
            product(x[:, :half], high[:half, :half], low[:half, :half], NT),
            product(x, high[half:], low[half:], NT),
        ],
        axis=1,
    )


def forward_step(s, source, before, m, w):
    if before is not None:
        source = source - lower(before, m[0].at[s - 1, 0], m[1].at[s - 1, 0])
    value = upper(source, w[0].at[s], w[1].at[s])
    return value, source - upper(value, m[0].at[s, 1], m[1].at[s, 1])


def first_kernel(mats, r, t, top):
    m, w = mats[:2], mats[2:4]
    value = None
    for s in range(8):
        value, t[s] = forward_step(s, r[s], value, m, w)
    z = upper_t(t[7], w[0][7], w[1][7])
    top[0] = z
    top[1] = lower(z, m[0][7, 0], m[1][7, 0])


def spread(out, kind, values, below, above):
    values = [below, *values, above]
    for s in range(8):
        for side in range(3):
            out[s, kind, side] = values[s + side]


def second_kernel(mats, t, top, z, above, ends):
    m, w = mats[:2], mats[2:4]
    value = top[0]
    values = {7: value}
    for s in range(6, -1, -1):
        above[s] = lower_t(value, m[0][s, 0], m[1][s, 0])
        value = upper_t(t[s] - above[s], w[0][s], w[1][s])
        values[s] = value
    above[7] = jnp.zeros_like(value)
    for s in range(8):
        z[s] = values[s]
    ends[:2] = top[...]
    ends[2] = value


def third_kernel(mats, r, t, z, above, source, t_left):
    m, g = mats[:2], mats[4:]
    for s in range(8):
        x = z[s]
        ahead = upper_t(x, m[0][s, 1], m[1][s, 1]) + above[s]
        own = [
            product(x[:, i * 128 : (i + 1) * 128], g[0][s, i], g[1][s, i], NN) for i in range(4)
        ]
        t_left[s] = t[s] - ahead
        source[s] = jnp.concatenate(own, axis=1) + ahead - t_left[s] - r[s]


def fourth_kernel(mats, source, t_left, from_below, from_above, t, last):
    m, w = mats[:2], mats[2:4]
    before = None
    for s in range(8):
        start = source[s]
        if s == 0:
            start = start + from_below[1]
        if s == 7:
            start = start + lower_t(from_above[2], m[0][7, 0], m[1][7, 0])
        before, more = forward_step(s, start, before, m, w)
        t[s] = t_left[s] + more
    last[...] = upper_t(t[7], w[0][7], w[1][7])


def fifth_kernel(mats, t, last, z, from_below, from_above, out):
    m, w = mats[:2], mats[2:4]
    value = last[...]
    values = [value]
    for s in range(6, -1, -1):
        ahead = lower_t(value, m[0][s, 0], m[1][s, 0])
        value = upper_t(t[s] - ahead, w[0][s], w[1][s])
        values.insert(0, value)
    zero = jnp.zeros_like(value)
    spread(out, 0, [z[s] for s in range(8)], from_below[0], from_above[2])
    spread(out, 1, values, zero, zero)


def halo_kernel(rows, *refs):
    out, odd = refs[-1], lax.axis_index("blk") % 2
    out[...] = rows[...]
    for n, got in enumerate(refs[:-1]):
        out[0, 1, 0] += got[...] * jnp.where(odd == n, 0.0, 1.0)


def place_rows(place, t, rhs, rows, lanes=slice(None)):
    count = rows.shape[0]
    place[pl.ds(pl.multiple_of((rhs ^ t) * count, count), count), lanes] = rows


def inner(a, b):
    return lax.dot_general(a, b, NT, precision=HIGHEST, preferred_element_type=F32)


def products_kernel(n, *refs):
    r_pieces, pieces, bands = refs[:n], refs[n : 2 * n], refs[2 * n : 2 * n + 4]
    r, d, q, e, w, under, sums, wide = refs[2 * n + 4 :]
    rhs, cells, total = lax.axis_index("rhs"), pieces[0].shape[4], r.shape[0]
    for t in range(n):
        place_rows(r, t, rhs, r_pieces[t][...])
        for kind in range(2):
            for side in range(3):
                rows = jnp.concatenate([pieces[t][j, kind, side] for j in range(SPAN)], axis=0)
                lanes = slice(side * cells, (side + 1) * cells)
                place_rows(wide.at[pl.ds(kind * total, total)], t, rhs, rows, lanes)
    below = along(wide[:, :cells], bands, 0, cells)
    image = below + along(wide[:, cells:], bands, cells, 3 * cells)
    first = jnp.where(lax.axis_index("pos") == 0, 1.0, 0.0)
    below_e = below[total:] * first
    own = slice(cells, 2 * cells)
    d[...], e[...] = wide[:total, own], wide[total:, own]
    q[...], w[...] = image[:total], image[total:]
    under[...] = wide[total:, :cells]
    odd = rhs % 2 == 1
    left = jnp.where(odd, e[...], d[...])
    rights = jnp.where(odd, q[...], r[...]), jnp.where(odd, w[...] + below_e, q[...])
    sums[...] = jnp.concatenate([inner(left, right) for right in rights], axis=1)


def small(a, b):
    return lax.dot_general(a, b, NN, precision=HIGHEST, preferred_element_type=F32)


def inverse(a):
    at = [lax.broadcasted_iota(jnp.int32, a.shape, d) for d in range(2)]
    same = at[0] == at[1]
    eye = jnp.where(same, 1.0, 0.0)
    kept = jnp.where(same, a, 0.0)
    by_row = lax.rsqrt(jnp.sum(kept, axis=1, keepdims=True))
    by_column = lax.rsqrt(jnp.sum(kept, axis=0, keepdims=True))
    a = a * by_row * by_column
    scale = 1.0 / jnp.max(jnp.sum(jnp.abs(a), axis=0, keepdims=True), axis=1, keepdims=True)
    rest = eye - a * scale
    total = eye + rest

    def step(total, rest):
        rest = product(rest, *halves(rest), NN)
        return total + product(total, *halves(rest), NN), rest

    for _ in range(7):
        total, rest = step(total, rest)

    def going(carry):
        turn, _, rest = carry
        return (turn < 40) & (jnp.max(jnp.abs(rest)) > 1e-7)

    def more(carry):
        turn, total, rest = carry
        return (turn + 1, *step(total, rest))

    _, total, _ = lax.while_loop(going, more, (jnp.int32(0), total, rest))
    total = total * scale
    total = total + small(total, eye - small(a, total))
    return total * by_row * by_column


def symmetric(a):
    return 0.5 * (a + a.T)


def last_kernel(own_sums, other_sums, r, d, q, e, w, arrived, *refs):
    bands, (solution, residual, all_weights) = refs[:4], refs[4:]
    count, total = solution.shape[0], r.shape[0]
    rhs = lax.axis_index("rhs")
    odd = rhs % 2 == 1
    sums = jnp.where(odd, other_sums[...], own_sums[...]), jnp.where(odd, own_sums[...], other_sums[...])
    s1, s2, s3, s4 = [
        symmetric(sums[k // 2][:, k % 2 * total : (k % 2 + 1) * total]) for k in range(4)
    ]
    gram = jnp.concatenate(
        [jnp.concatenate([s2, s3], axis=1), jnp.concatenate([s3, s4], axis=1)], axis=0
    )
    weights = small(jnp.concatenate([s1, s2 - s1], axis=1), inverse(gram))
    all_weights[...] = weights
    weights = all_weights[pl.ds(pl.multiple_of(rhs * count, count), count), :]
    own = r[pl.ds(pl.multiple_of(rhs * count, count), count), :]
    solution[...] = small(weights, jnp.concatenate([d[...], e[...]], axis=0))
    cells, last = own.shape[1], lax.axis_index("pos") == SPAN - 1
    above = along(arrived[...] * jnp.where(last, 1.0, 0.0), bands, 2 * cells, 3 * cells)
    residual[...] = own - small(weights, jnp.concatenate([q[...], w[...] + above], axis=0))


def swapped(value, axis, bit):
    return lax.ppermute(value, axis, [(i, i ^ bit) for i in range(lax.axis_size(axis))])


def summed(value):
    axes = ("blk", "pos")
    size = lax.axis_size(axes)
    bit = 1
    while bit < size:
        near = value + swapped(value, axes, bit)
        if 2 * bit < size:
            near = near + (swapped(value, axes, 2 * bit) + swapped(value, axes, 3 * bit))
        value = near
        bit *= 4
    return value


def exchanged(value):
    blocks, got = lax.axis_size("blk"), []
    for first in range(min(2, blocks - 1)):
        pairs = [(i, i + 1) for i in range(first, blocks - 1, 2)]
        got.append(lax.ppermute(value, "blk", pairs + [(b, a) for a, b in pairs]))
    return got


def both_ways(value):
    low = high = None
    for first, got in enumerate(exchanged(value)):
        even = lax.axis_index("blk") % 2 == first
        up, down = jnp.where(even, 0.0, got), jnp.where(even, got, 0.0)
        low, high = (up, down) if low is None else (low + up, high + down)
    return low, high


def shards(right_side, tiles, pivots, columns):
    count, cells = right_side.shape
    shard_rows, slots, order, _ = tiles.shape
    parts = lax.axis_size("rhs")
    blocks = lax.axis_size("blk")
    rows_part = shard_rows // parts
    each = count // SPAN
    total = count * parts
    S = jax.ShapeDtypeStruct
    edges = [(SPAN * i - 1, SPAN * i + 1) for i in range(1, blocks)]

    def others(value):
        return [value] + [swapped(value, "rhs", t) for t in range(1, parts)]

    tall = 2 * order + 8
    own, part, offsets = call(
        functools.partial(pack_kernel, rows_part),
        "pack_tiles",
        [
            pltpu.VMEM((shard_rows, tall, 2 * order), F32),
            S((rows_part, tall, 2 * order), F32),
            S((1, 3), jnp.int32),
        ],
        [pl.BlockSpec(memory_space=pl.ANY)] * 3,
        [VMEM, VMEM, SMEM],
        [
            pltpu.SMEM(columns.shape, jnp.int32),
            pltpu.VMEM(tiles.shape, F32),
            pltpu.VMEM(pivots.shape, F32),
            pltpu.SemaphoreType.DMA((2 + shard_rows,)),
        ],
        cost=2,
        limit=60,
    )(columns, tiles, pivots)

    vectors, vector = S((SPAN, each, cells), F32), S((each, cells), F32)
    r = lax.all_to_all(right_side.reshape(SPAN, each, cells), "pos", 0, 0, tiled=True)
    x, y, z = (swapped(part, "pos", bit) for bit in (1, 2, 4))
    mat_shapes = [
        pltpu.VMEM((SPAN, 2, cells, cells), BF16),
        pltpu.VMEM((SPAN, 2, cells, cells), BF16),
        pltpu.VMEM((SPAN, cells, cells), BF16),
        pltpu.VMEM((SPAN, cells, cells), BF16),
        pltpu.VMEM((SPAN, 4, 2 * order, 2 * order), BF16),
        pltpu.VMEM((SPAN, 4, 2 * order, 2 * order), BF16),
    ]
    splits = lambda groups: pltpu.VMEM((groups, 2, 8, 2, 2, order, 2 * order), BF16)
    bands = []
    for half in range(2):
        bands += call(
            functools.partial(band_kernel, half * shard_rows // 2),
            "row_band",
            [S((3 * cells, cells // 2), BF16)] * 2,
            [SMEM, VMEM],
            [VMEM] * 2,
            [pltpu.VMEM((3 * cells, cells // 2), F32)],
            cost=20,
        )(columns, tiles)

    own, r = lax.optimization_barrier((own, r))
    mats = call(
        own_factor_kernel,
        "factors_own",
        mat_shapes,
        [SMEM, VMEM],
        [VMEM] * 6,
        [splits(1)],
        cost=4,
    )(offsets, own)
    def with_mats(kernel, name, specs, out_shapes, given, scratch=(), cost=1):
        nonlocal mats
        first, outs = len(given), len(out_shapes)

        def body(*refs):
            ins, rest = refs[:first], refs[first + 6 :]
            kernel(ins, rest[outs : outs + 6], rest[:outs], rest[outs + 6 :])

        *results, m0, m1, w0, w1, g0, g1 = call(
            body,
            name,
            [*out_shapes, *mat_shapes],
            [*specs, *[VMEM] * 6],
            [VMEM] * (outs + 6),
            scratch,
            {first + i: outs + i for i in range(6)},
            cost,
        )(*given, *mats)
        mats = [m0, m1, w0, w1, g0, g1]
        return results

    def add_factors(name, layout, operands, cost):
        given = [offsets] + [piece for operand in operands for piece in others(operand)]
        with_mats(
            functools.partial(factor_kernel, layout, parts),
            name,
            [SMEM] + [VMEM] * (len(given) - 1),
            [],
            given,
            [pltpu.VMEM((len(layout), shard_rows, tall, 2 * order), F32), splits(len(layout))],
            cost,
        )

    def sweep(kernel, name, out_shapes, *given, cost=1):
        def body(ins, held, outs, scratch):
            kernel(held, *ins, *outs)

        return with_mats(body, name, [VMEM] * len(given), out_shapes, given, cost=cost)

    join = lambda *pieces: jnp.concatenate(pieces, axis=1)
    xs = swapped(join(y[:, :order], z[:, :order]), "pos", 1)
    ys = swapped(join(x[:, order:], z[:, :order]), "pos", 2)
    zs = swapped(join(x[:, order:], y[:, order:]), "pos", 4)
    rest = tall - order
    far_top = swapped(ys[:, rest:], "pos", 1)
    far_low = swapped(ys[:, :rest], "pos", 4)
    add_factors(
        "factors_near", [(bit, [(i, 0, tall)]) for i, bit in enumerate((1, 2, 4))], [x, y, z], 6
    )
    add_factors(
        "factors_mid",
        [
            (3, [(0, 0, order), (1, 0, rest)]),
            (5, [(0, order, order), (2, 0, rest)]),
            (6, [(1, rest, order), (2, rest, rest)]),
        ],
        [xs, ys, zs],
        6,
    )
    add_factors("factors_far", [(7, [(0, 0, order), (1, 0, rest)])], [far_top, far_low], 3)

    r_pieces = others(right_side)
    ends_shape, spread_shape = S((3, each, cells), F32), S((SPAN, 2, 3, each, cells), F32)
    t, top = sweep(first_kernel, "forward_r", [vectors, S((2, each, cells), F32)], r, cost=4)
    z, above, ends = sweep(
        second_kernel, "backward_r", [vectors, vectors, ends_shape], t, top, cost=4
    )
    from_below, from_above = both_ways(ends)
    source, t_left = sweep(third_kernel, "residue_of_z", [vectors] * 2, r, t, z, above, cost=2)
    t, last = sweep(
        fourth_kernel, "forward_v", [vectors, vector], source, t_left, from_below, from_above, cost=4
    )
    halos = exchanged(last)
    (rows,) = sweep(
        fifth_kernel, "backward_v", [spread_shape], t, last, z, from_below, from_above, cost=4
    )
    rows = call(halo_kernel, "halo", spread_shape, [VMEM] * (1 + len(halos)))(rows, *halos)
    rows = lax.all_to_all(rows, "pos", 0, 0, tiled=True)

    full, sums_shape = S((total, cells), F32), S((total, 2 * total), F32)
    r_full, d, q, e, w, under, sums = call(
        functools.partial(products_kernel, parts),
        "products",
        [full] * 6 + [sums_shape],
        [VMEM] * (2 * parts + 4),
        [VMEM] * 7,
        [pltpu.VMEM((2 * total, 3 * cells), F32)],
        cost=2,
    )(*r_pieces, *others(rows), *bands)
    sums = summed(sums)
    e_above = lax.ppermute(under, ("blk", "pos"), edges + [(b, a) for a, b in edges])
    return call(
        last_kernel,
        "update",
        [S((count, cells), F32)] * 2,
        [VMEM] * 12,
        [VMEM] * 2,
        [pltpu.VMEM((total, 2 * total), F32)],
        cost=4,
    )(sums, swapped(sums, "rhs", 1), r_full, d, q, e, w, e_above, *bands)


def solution(mesh):
    devices = mesh.devices
    split = Mesh(
        devices.reshape(devices.shape[0] // SPAN, SPAN, devices.shape[1]), ("blk", "pos", "rhs")
    )
    rows = ("blk", "pos")
    return jax.shard_map(
        shards,
        mesh=split,
        in_specs=(
            P("rhs", rows),
            P(rows, None, None, None),
            P(rows, None, None),
            P(rows, None),
        ),
        out_specs=(P("rhs", rows), P("rhs", rows)),
        check_vma=False,
    )
```

```python
import functools
import jax
import jax.numpy as jnp
from jax import lax
from jax.experimental import pallas as pl
from jax.experimental.pallas import tpu as pltpu
from jax.sharding import Mesh, PartitionSpec as P

SPAN = 8
F32 = jnp.float32
BF16 = jnp.bfloat16
HIGHEST = lax.Precision.HIGHEST
NN = (((1,), (0,)), ((), ()))
NT = (((1,), (1,)), ((), ()))
VMEM = pl.BlockSpec(memory_space=pltpu.VMEM)
SMEM = pl.BlockSpec(memory_space=pltpu.SMEM)


def call(kernel, name, out_shape, in_specs, out_specs=VMEM, scratch=(), aliases=None, cost=1, limit=16):
    return pl.pallas_call(
        kernel,
        out_shape=out_shape,
        in_specs=in_specs,
        out_specs=out_specs,
        scratch_shapes=list(scratch),
        input_output_aliases=aliases or {},
        cost_estimate=pl.CostEstimate(flops=int(cost * 1e9), bytes_accessed=0, transcendentals=0),
        compiler_params=pltpu.CompilerParams(vmem_limit_bytes=limit * 2**20),
        name=name,
    )


def two_parts(x):
    high = x.astype(BF16).astype(F32)
    return jnp.concatenate([high, x - high], axis=0).astype(BF16)


def halves(x):
    high = x.astype(BF16)
    return high, (x - high.astype(F32)).astype(BF16)


def product(x, high, low, dims):
    parts = two_parts(x)
    both = lax.dot_general(parts, high, dims, preferred_element_type=F32)
    both = both + lax.dot_general(parts, low, dims, preferred_element_type=F32)
    rows = x.shape[0]
    return both[:rows] + both[rows:]


def offsets_of(columns, start):
    found = []
    for offset in range(1, 8):
        hit = jnp.int32(0)
        for slot in range(7):
            away = columns[0, slot] - start
            hit = hit | jnp.where((away == offset) | (away == -offset), 1, 0)
        found.append(hit * 16 + offset)
    first = functools.reduce(jnp.maximum, found)
    second = functools.reduce(jnp.maximum, [jnp.where(f == first, 0, f) for f in found])
    first, second = (first & 15, second & 15)
    return (jnp.minimum(first, second), jnp.maximum(first, second), jnp.int32(8))


def pack_kernel(rows_part, columns_far, tiles_far, pivots_far, own, part, offsets, *scratch):
    columns, tiles, pivots, sems = scratch
    shard_rows, slots, order, _ = tiles.shape
    copies = [
        pltpu.make_async_copy(far, near, sems.at[i])
        for i, (far, near) in enumerate(((columns_far, columns), (pivots_far, pivots)))
    ]
    for row in range(shard_rows):
        copies.append(pltpu.make_async_copy(tiles_far.at[row], tiles.at[row], sems.at[2 + row]))
    for copy in copies:
        copy.start()
    copies[0].wait()
    start = (lax.axis_index("blk") * SPAN + lax.axis_index("pos")) * shard_rows
    offs = offsets_of(columns, start)
    for k in range(3):
        offsets[0, k] = offs[k]
    at = [lax.broadcasted_iota(jnp.int32, (order, order), d) for d in range(2)]
    copies[1].wait()
    for row in range(shard_rows):
        copies[2 + row].wait()
        sums = [jnp.zeros((order, order), F32) for _ in range(4)]
        for slot in range(slots):
            away = columns[row, slot] - (start + row)
            tile = tiles[row, slot]
            for k, want in enumerate((*offs, 0)):
                sums[k] = sums[k] + tile * jnp.where(away == want, 1.0, 0.0)
        both = jnp.where(at[0] <= at[1], pivots[row], sums[3])
        line = jnp.sum(jnp.where(at[0] == at[1], sums[3], 0.0), axis=0, keepdims=True)
        own[row, :order] = jnp.concatenate([sums[0], sums[1]], axis=1)
        own[row, order : 2 * order] = jnp.concatenate([sums[2], both], axis=1)
        own[row, 2 * order :] = jnp.broadcast_to(jnp.concatenate([line, line], axis=1), (8, 2 * order))
    for a in range(rows_part):
        part[a] = own[lax.axis_index("rhs") * rows_part + a]


def band_kernel(first_row, columns, tiles, band_high, band_low, band):
    shard_rows, slots, order, _ = tiles.shape
    start = (lax.axis_index("blk") * SPAN + lax.axis_index("pos")) * shard_rows
    band[...] = jnp.zeros_like(band)
    for row in range(shard_rows // 2):
        for slot in range(slots):
            away = columns[first_row + row, slot] - start + shard_rows
            where = pl.ds(pl.multiple_of(away * order, order), order)
            lanes = pl.ds(row * order, order)
            band[where, lanes] = band[where, lanes] + tiles[first_row + row, slot].T
    high, low = halves(band[...])
    band_high[...] = high
    band_low[...] = low


def along(x, bands, first, last):
    return jnp.concatenate(
        [product(x, high[first:last], low[first:last], NN) for high, low in zip(bands[::2], bands[1::2])],
        axis=1,
    )


def stage_rows(stage, t, pieces):
    rows_part = pieces[0][0].shape[0]
    base = (lax.axis_index("rhs") ^ t) * rows_part
    for r in range(rows_part):
        top = 0
        for ref, first, rows in pieces:
            stage[base + r, top : top + rows] = ref[r, first : first + rows]
            top += rows


def factors(offsets, stages, split, groups, m_high, m_low, w_high, w_low, g_high, g_low):
    order = 64
    o = [offsets[0, k] for k in range(3)]
    at = [lax.broadcasted_iota(jnp.int32, (order, order), d) for d in range(2)]
    lane = lax.broadcasted_iota(jnp.int32, (order, 2 * order), 1)
    pivots, lefts = {}, {}
    for n, (stage, s) in enumerate(zip(stages, groups)):
        for i in range(8):
            for p in range(2):
                pair = stage[i, p * order : (p + 1) * order]
                turned = jnp.concatenate([pair[:, order:], pair[:, :order]], axis=1)
                for version, tiles in enumerate((pair, turned)):
                    split[n, 0, i, version, p], split[n, 1, i, version, p] = halves(tiles)
            both = stage[i, order : 2 * order, order:]
            turned = both.T
            pivots[n, i] = jnp.where(at[0] <= at[1], both, turned)
            line = stage[i, 2 * order : 2 * order + 1, :order]
            tile = jnp.where(at[0] > at[1], both, jnp.where(at[0] < at[1], turned, line))
            high, low = halves(tile)
            where = slice(i % 2 * order, (i % 2 + 1) * order)
            g_high[s, i // 2, where, where] = high
            g_low[s, i // 2, where, where] = low
        for j in range(7):
            inside = [jnp.where(o[k] + j <= 7, 1.0, 0.0) for k in range(2)]
            pair = stage[j, :order] * jnp.where(lane < order, inside[0], inside[1])
            left = two_parts(product(pivots[n, j], *halves(pair), NN))
            lefts[n, j] = jnp.concatenate([left, left], axis=1)
        for i in range(8):
            lanes = slice(i * order, (i + 1) * order)
            side = slice(i % 2 * order, (i % 2 + 1) * order)
            for k in range(3):
                from_row = (i - o[k]) & 7 if k < 2 else i
                kind = jnp.where(o[k] > i, 0, 1) if k < 2 else 0
                where = pl.ds(pl.multiple_of(from_row * order, order), order)
                for part, m in enumerate((m_high, m_low)):
                    m[s, kind, where, lanes] = split[n, part, from_row, (i + k) % 2, k // 2, :, side]
    for j in range(7, -1, -1):
        first = j // 2 * 128
        for n, s in enumerate(groups):
            after = 8 * order - first - (j % 2 + 1) * order
            row = jnp.pad(pivots[n, j], ((0, 0), (j % 2 * order, after)))
            if j < 7:
                where = [
                    pl.ds(pl.multiple_of(jnp.minimum(o[k] + j, 7) * order, order), order)
                    for k in range(2)
                ]
                right = jnp.concatenate(
                    [w[s, where[k], first:] for w in (w_high, w_low) for k in range(2)], axis=0
                )
                both = lax.dot_general(lefts[n, j], right, NN, preferred_element_type=F32)
                row = row - (both[:order] + both[order:])
            high, low = halves(row)
            w_high[s, j * order : (j + 1) * order, first:] = high
            w_low[s, j * order : (j + 1) * order, first:] = low


def own_factor_kernel(offsets, own, m_high, m_low, w_high, w_low, g_high, g_low, split):
    mats = (m_high, m_low, w_high, w_low, g_high, g_low)
    half = m_high.shape[2] // 2
    for ref in (m_high, m_low):
        for kind in range(2):
            ref[:, kind, :half, : half * (1 + kind)] = jnp.zeros((SPAN, half, half * (1 + kind)), BF16)
            ref[:, kind, half:, half * kind :] = jnp.zeros((SPAN, half, half * (2 - kind)), BF16)
    for ref in mats[2:]:
        ref[...] = jnp.zeros_like(ref)
    factors(offsets, [own], split, [lax.axis_index("pos")], *mats)


def factor_kernel(layout, count, ins, mats, outs, scratch):
    offsets, given = ins[0], ins[1:]
    staged, groups = [], []
    for n, (mask, pieces) in enumerate(layout):
        stage = scratch[0].at[n]
        for t in range(count):
            stage_rows(stage, t, [(given[i * count + t], first, rows) for i, first, rows in pieces])
        staged.append(stage)
        groups.append(lax.axis_index("pos") ^ mask)
    factors(offsets, staged, scratch[1], groups, *mats)


def upper(x, high, low):
    half = high.shape[0] // 2
    return jnp.concatenate(
        [
            product(x[:, :half], high[:half, :half], low[:half, :half], NN),
            product(x, high[:, half:], low[:, half:], NN),
        ],
        axis=1,
    )


def upper_t(x, high, low):
    half = high.shape[0] // 2
    return jnp.concatenate(
        [
            product(x, high[:half], low[:half], NT),
            product(x[:, half:], high[half:, half:], low[half:, half:], NT),
        ],
        axis=1,
    )


def lower(x, high, low):
    half = high.shape[0] // 2
    return jnp.concatenate(
        [
            product(x, high[:, :half], low[:, :half], NN),
            product(x[:, half:], high[half:, half:], low[half:, half:], NN),
        ],
        axis=1,
    )


def lower_t(x, high, low):
    half = high.shape[0] // 2
    return jnp.concatenate(
        [
            product(x[:, :half], high[:half, :half], low[:half, :half], NT),
            product(x, high[half:], low[half:], NT),
        ],
        axis=1,
    )


def forward_step(s, source, before, m, w):
    if before is not None:
        source = source - lower(before, m[0].at[s - 1, 0], m[1].at[s - 1, 0])
    value = upper(source, w[0].at[s], w[1].at[s])
    return value, source - upper(value, m[0].at[s, 1], m[1].at[s, 1])


def first_kernel(mats, r, t, top):
    m, w = mats[:2], mats[2:4]
    value = None
    for s in range(8):
        value, t[s] = forward_step(s, r[s], value, m, w)
    z = upper_t(t[7], w[0][7], w[1][7])
    top[0] = z
    top[1] = lower(z, m[0][7, 0], m[1][7, 0])


def spread(out, kind, values, below, above):
    values = [below, *values, above]
    for s in range(8):
        for side in range(3):
            out[s, kind, side] = values[s + side]


def second_kernel(mats, t, top, z, above, ends):
    m, w = mats[:2], mats[2:4]
    value = top[0]
    values = {7: value}
    for s in range(6, -1, -1):
        above[s] = lower_t(value, m[0][s, 0], m[1][s, 0])
        value = upper_t(t[s] - above[s], w[0][s], w[1][s])
        values[s] = value
    above[7] = jnp.zeros_like(value)
    for s in range(8):
        z[s] = values[s]
    ends[:2] = top[...]
    ends[2] = value


def third_kernel(mats, r, t, z, above, source, t_left):
    m, g = mats[:2], mats[4:]
    for s in range(8):
        x = z[s]
        ahead = upper_t(x, m[0][s, 1], m[1][s, 1]) + above[s]
        own = [
            product(x[:, i * 128 : (i + 1) * 128], g[0][s, i], g[1][s, i], NN) for i in range(4)
        ]
        t_left[s] = t[s] - ahead
        source[s] = jnp.concatenate(own, axis=1) + ahead - t_left[s] - r[s]


def fourth_kernel(mats, source, t_left, from_below, from_above, t, last):
    m, w = mats[:2], mats[2:4]
    before = None
    for s in range(8):
        start = source[s]
        if s == 0:
            start = start + from_below[1]
        if s == 7:
            start = start + lower_t(from_above[2], m[0][7, 0], m[1][7, 0])
        before, more = forward_step(s, start, before, m, w)
        t[s] = t_left[s] + more
    last[...] = upper_t(t[7], w[0][7], w[1][7])


def fifth_kernel(mats, t, last, z, from_below, from_above, out):
    m, w = mats[:2], mats[2:4]
    value = last[...]
    values = [value]
    for s in range(6, -1, -1):
        ahead = lower_t(value, m[0][s, 0], m[1][s, 0])
        value = upper_t(t[s] - ahead, w[0][s], w[1][s])
        values.insert(0, value)
    zero = jnp.zeros_like(value)
    spread(out, 0, [z[s] for s in range(8)], from_below[0], from_above[2])
    spread(out, 1, values, zero, zero)


def halo_kernel(rows, *refs):
    out, odd = refs[-1], lax.axis_index("blk") % 2
    out[...] = rows[...]
    for n, got in enumerate(refs[:-1]):
        out[0, 1, 0] += got[...] * jnp.where(odd == n, 0.0, 1.0)


def place_rows(place, t, rhs, rows, lanes=slice(None)):
    count = rows.shape[0]
    place[pl.ds(pl.multiple_of((rhs ^ t) * count, count), count), lanes] = rows


def inner(a, b):
    return lax.dot_general(a, b, NT, precision=HIGHEST, preferred_element_type=F32)


def products_kernel(n, *refs):
    r_pieces, pieces, bands = refs[:n], refs[n : 2 * n], refs[2 * n : 2 * n + 4]
    r, d, q, e, w, under, sums, wide = refs[2 * n + 4 :]
    rhs, cells, total = lax.axis_index("rhs"), pieces[0].shape[4], r.shape[0]
    for t in range(n):
        place_rows(r, t, rhs, r_pieces[t][...])
        for kind in range(2):
            for side in range(3):
                rows = jnp.concatenate([pieces[t][j, kind, side] for j in range(SPAN)], axis=0)
                lanes = slice(side * cells, (side + 1) * cells)
                place_rows(wide.at[pl.ds(kind * total, total)], t, rhs, rows, lanes)
    below = along(wide[:, :cells], bands, 0, cells)
    image = below + along(wide[:, cells:], bands, cells, 3 * cells)
    first = jnp.where(lax.axis_index("pos") == 0, 1.0, 0.0)
    below_e = below[total:] * first
    own = slice(cells, 2 * cells)
    d[...], e[...] = wide[:total, own], wide[total:, own]
    q[...], w[...] = image[:total], image[total:]
    under[...] = wide[total:, :cells]
    odd = rhs % 2 == 1
    left = jnp.where(odd, e[...], d[...])
    rights = jnp.where(odd, q[...], r[...]), jnp.where(odd, w[...] + below_e, q[...])
    sums[...] = jnp.concatenate([inner(left, right) for right in rights], axis=1)


def small(a, b):
    return lax.dot_general(a, b, NN, precision=HIGHEST, preferred_element_type=F32)


def inverse(a):
    at = [lax.broadcasted_iota(jnp.int32, a.shape, d) for d in range(2)]
    same = at[0] == at[1]
    eye = jnp.where(same, 1.0, 0.0)
    kept = jnp.where(same, a, 0.0)
    by_row = lax.rsqrt(jnp.sum(kept, axis=1, keepdims=True))
    by_column = lax.rsqrt(jnp.sum(kept, axis=0, keepdims=True))
    a = a * by_row * by_column
    scale = 1.0 / jnp.max(jnp.sum(jnp.abs(a), axis=0, keepdims=True), axis=1, keepdims=True)
    rest = eye - a * scale
    total = eye + rest

    def step(total, rest):
        rest = product(rest, *halves(rest), NN)
        return total + product(total, *halves(rest), NN), rest

    for _ in range(7):
        total, rest = step(total, rest)

    def going(carry):
        turn, _, rest = carry
        return (turn < 40) & (jnp.max(jnp.abs(rest)) > 1e-7)

    def more(carry):
        turn, total, rest = carry
        return (turn + 1, *step(total, rest))

    _, total, _ = lax.while_loop(going, more, (jnp.int32(0), total, rest))
    total = total * scale
    total = total + small(total, eye - small(a, total))
    return total * by_row * by_column


def symmetric(a):
    return 0.5 * (a + a.T)


def last_kernel(own_sums, other_sums, r, d, q, e, w, arrived, *refs):
    bands, (solution, residual, all_weights) = refs[:4], refs[4:]
    count, total = solution.shape[0], r.shape[0]
    rhs = lax.axis_index("rhs")
    odd = rhs % 2 == 1
    sums = jnp.where(odd, other_sums[...], own_sums[...]), jnp.where(odd, own_sums[...], other_sums[...])
    s1, s2, s3, s4 = [
        symmetric(sums[k // 2][:, k % 2 * total : (k % 2 + 1) * total]) for k in range(4)
    ]
    gram = jnp.concatenate(
        [jnp.concatenate([s2, s3], axis=1), jnp.concatenate([s3, s4], axis=1)], axis=0
    )
    weights = small(jnp.concatenate([s1, s2 - s1], axis=1), inverse(gram))
    all_weights[...] = weights
    weights = all_weights[pl.ds(pl.multiple_of(rhs * count, count), count), :]
    own = r[pl.ds(pl.multiple_of(rhs * count, count), count), :]
    solution[...] = small(weights, jnp.concatenate([d[...], e[...]], axis=0))
    cells, last = own.shape[1], lax.axis_index("pos") == SPAN - 1
    above = along(arrived[...] * jnp.where(last, 1.0, 0.0), bands, 2 * cells, 3 * cells)
    residual[...] = own - small(weights, jnp.concatenate([q[...], w[...] + above], axis=0))


def swapped(value, axis, bit):
    return lax.ppermute(value, axis, [(i, i ^ bit) for i in range(lax.axis_size(axis))])


def summed(value):
    axes = ("blk", "pos")
    size = lax.axis_size(axes)
    bit = 1
    while bit < size:
        near = value + swapped(value, axes, bit)
        if 2 * bit < size:
            near = near + (swapped(value, axes, 2 * bit) + swapped(value, axes, 3 * bit))
        value = near
        bit *= 4
    return value


def exchanged(value):
    blocks, got = lax.axis_size("blk"), []
    for first in range(min(2, blocks - 1)):
        pairs = [(i, i + 1) for i in range(first, blocks - 1, 2)]
        got.append(lax.ppermute(value, "blk", pairs + [(b, a) for a, b in pairs]))
    return got


def both_ways(value):
    low = high = None
    for first, got in enumerate(exchanged(value)):
        even = lax.axis_index("blk") % 2 == first
        up, down = jnp.where(even, 0.0, got), jnp.where(even, got, 0.0)
        low, high = (up, down) if low is None else (low + up, high + down)
    return low, high


def shards(right_side, tiles, pivots, columns):
    count, cells = right_side.shape
    shard_rows, slots, order, _ = tiles.shape
    parts = lax.axis_size("rhs")
    blocks = lax.axis_size("blk")
    rows_part = shard_rows // parts
    each = count // SPAN
    total = count * parts
    S = jax.ShapeDtypeStruct
    edges = [(SPAN * i - 1, SPAN * i + 1) for i in range(1, blocks)]

    def others(value):
        return [value] + [swapped(value, "rhs", t) for t in range(1, parts)]

    tall = 2 * order + 8
    own, part, offsets = call(
        functools.partial(pack_kernel, rows_part),
        "pack_tiles",
        [
            pltpu.VMEM((shard_rows, tall, 2 * order), F32),
            pltpu.VMEM((rows_part, tall, 2 * order), F32),
            S((1, 3), jnp.int32),
        ],
        [pl.BlockSpec(memory_space=pl.ANY)] * 3,
        [VMEM, VMEM, SMEM],
        [
            pltpu.SMEM(columns.shape, jnp.int32),
            pltpu.VMEM(tiles.shape, F32),
            pltpu.VMEM(pivots.shape, F32),
            pltpu.SemaphoreType.DMA((2 + shard_rows,)),
        ],
        cost=2,
        limit=60,
    )(columns, tiles, pivots)

    vectors, vector = S((SPAN, each, cells), F32), S((each, cells), F32)
    r = lax.all_to_all(right_side.reshape(SPAN, each, cells), "pos", 0, 0, tiled=True)
    x, y, z = (swapped(part, "pos", bit) for bit in (1, 2, 4))
    mat_shapes = [
        pltpu.VMEM((SPAN, 2, cells, cells), BF16),
        pltpu.VMEM((SPAN, 2, cells, cells), BF16),
        pltpu.VMEM((SPAN, cells, cells), BF16),
        pltpu.VMEM((SPAN, cells, cells), BF16),
        pltpu.VMEM((SPAN, 4, 2 * order, 2 * order), BF16),
        pltpu.VMEM((SPAN, 4, 2 * order, 2 * order), BF16),
    ]
    splits = lambda groups: pltpu.VMEM((groups, 2, 8, 2, 2, order, 2 * order), BF16)
    bands = []
    for half in range(2):
        bands += call(
            functools.partial(band_kernel, half * shard_rows // 2),
            "row_band",
            [S((3 * cells, cells // 2), BF16)] * 2,
            [SMEM, VMEM],
            [VMEM] * 2,
            [pltpu.VMEM((3 * cells, cells // 2), F32)],
            cost=20,
        )(columns, tiles)

    own, r = lax.optimization_barrier((own, r))
    mats = call(
        own_factor_kernel,
        "factors_own",
        mat_shapes,
        [SMEM, VMEM],
        [VMEM] * 6,
        [splits(1)],
        cost=4,
    )(offsets, own)
    def with_mats(kernel, name, specs, out_shapes, given, scratch=(), cost=1):
        nonlocal mats
        first, outs = len(given), len(out_shapes)

        def body(*refs):
            ins, rest = refs[:first], refs[first + 6 :]
            kernel(ins, rest[outs : outs + 6], rest[:outs], rest[outs + 6 :])

        *results, m0, m1, w0, w1, g0, g1 = call(
            body,
            name,
            [*out_shapes, *mat_shapes],
            [*specs, *[VMEM] * 6],
            [VMEM] * (outs + 6),
            scratch,
            {first + i: outs + i for i in range(6)},
            cost,
        )(*given, *mats)
        mats = [m0, m1, w0, w1, g0, g1]
        return results

    def add_factors(name, layout, operands, cost):
        given = [offsets] + [piece for operand in operands for piece in others(operand)]
        with_mats(
            functools.partial(factor_kernel, layout, parts),
            name,
            [SMEM] + [VMEM] * (len(given) - 1),
            [],
            given,
            [pltpu.VMEM((len(layout), shard_rows, tall, 2 * order), F32), splits(len(layout))],
            cost,
        )

    def sweep(kernel, name, out_shapes, *given, cost=1):
        def body(ins, held, outs, scratch):
            kernel(held, *ins, *outs)

        return with_mats(body, name, [VMEM] * len(given), out_shapes, given, cost=cost)

    join = lambda *pieces: jnp.concatenate(pieces, axis=1)
    xs = swapped(join(y[:, :order], z[:, :order]), "pos", 1)
    ys = swapped(join(x[:, order:], z[:, :order]), "pos", 2)
    zs = swapped(join(x[:, order:], y[:, order:]), "pos", 4)
    rest = tall - order
    far_top = swapped(ys[:, rest:], "pos", 1)
    far_low = swapped(ys[:, :rest], "pos", 4)
    add_factors(
        "factors_near", [(bit, [(i, 0, tall)]) for i, bit in enumerate((1, 2, 4))], [x, y, z], 6
    )
    add_factors(
        "factors_mid",
        [
            (3, [(0, 0, order), (1, 0, rest)]),
            (5, [(0, order, order), (2, 0, rest)]),
            (6, [(1, rest, order), (2, rest, rest)]),
        ],
        [xs, ys, zs],
        6,
    )
    add_factors("factors_far", [(7, [(0, 0, order), (1, 0, rest)])], [far_top, far_low], 3)

    r_pieces = others(right_side)
    ends_shape, spread_shape = S((3, each, cells), F32), S((SPAN, 2, 3, each, cells), F32)
    t, top = sweep(first_kernel, "forward_r", [vectors, S((2, each, cells), F32)], r, cost=4)
    z, above, ends = sweep(
        second_kernel, "backward_r", [vectors, vectors, ends_shape], t, top, cost=4
    )
    from_below, from_above = both_ways(ends)
    source, t_left = sweep(third_kernel, "residue_of_z", [vectors] * 2, r, t, z, above, cost=2)
    t, last = sweep(
        fourth_kernel, "forward_v", [vectors, vector], source, t_left, from_below, from_above, cost=4
    )
    halos = exchanged(last)
    (rows,) = sweep(
        fifth_kernel, "backward_v", [spread_shape], t, last, z, from_below, from_above, cost=4
    )
    rows = call(halo_kernel, "halo", spread_shape, [VMEM] * (1 + len(halos)))(rows, *halos)
    rows = lax.all_to_all(rows, "pos", 0, 0, tiled=True)

    full, sums_shape = S((total, cells), F32), S((total, 2 * total), F32)
    r_full, d, q, e, w, under, sums = call(
        functools.partial(products_kernel, parts),
        "products",
        [full] * 6 + [sums_shape],
        [VMEM] * (2 * parts + 4),
        [VMEM] * 7,
        [pltpu.VMEM((2 * total, 3 * cells), F32)],
        cost=2,
    )(*r_pieces, *others(rows), *bands)
    sums = summed(sums)
    e_above = lax.ppermute(under, ("blk", "pos"), edges + [(b, a) for a, b in edges])
    return call(
        last_kernel,
        "update",
        [S((count, cells), F32)] * 2,
        [VMEM] * 12,
        [VMEM] * 2,
        [pltpu.VMEM((total, 2 * total), F32)],
        cost=4,
    )(sums, swapped(sums, "rhs", 1), r_full, d, q, e, w, e_above, *bands)


def solution(mesh):
    devices = mesh.devices
    split = Mesh(
        devices.reshape(devices.shape[0] // SPAN, SPAN, devices.shape[1]), ("blk", "pos", "rhs")
    )
    rows = ("blk", "pos")
    return jax.shard_map(
        shards,
        mesh=split,
        in_specs=(
            P("rhs", rows),
            P(rows, None, None, None),
            P(rows, None, None),
            P(rows, None),
        ),
        out_specs=(P("rhs", rows), P("rhs", rows)),
        check_vma=False,
    )
```
